128 devices in a mesh: attn: 16 (over y, z), ffn: 8 (over x, core).
Axes of the slice: x: 4, y: 4, z: 4, core: 2. Of those that a mesh axis runs over, the one named last changes fastest.
Arguments:
- stream: bfloat16 [512, 16384], P(None, 'attn'), may hold values from -12 to 12
- queries: bfloat16 [512, 16384], P('attn', 'ffn'), may hold values from -16 to 16
- k_pool: bfloat16 [4096, 16, 1024], P('attn', None, 'ffn'), may hold values from -6 to 6
- v_pool: bfloat16 [4096, 16, 1024], P('attn', None, 'ffn'), may hold values from -24 to 24
- page_table: int32 [512, 32], replicated, may hold values from 0 to 255, as said below
- lengths: int32 [512], replicated, may hold values from 1 to 512
- home_device: int32 [512, 1], replicated, may hold values from 0 to 15; in each aligned block of 32 rows (0 to 31, 32 to 63, ...) at most 4 rows name the same one
- w_out: bfloat16 [16384, 16384], P('ffn', 'attn'), may hold values from -0.046875 to 0.046875
- norm_gain: bfloat16 [16384], P('attn'), may hold values from 0.099609375 to 1.8984375
- w_gate: bfloat16 [16384, 26624], P('attn', 'ffn'), may hold values from -0.046875 to 0.046875
- w_up: bfloat16 [16384, 26624], P('attn', 'ffn'), may hold values from -0.046875 to 0.046875
Outputs:
- residual: bfloat16 [512, 16384], P(None, 'attn')
- hidden: bfloat16 [512, 26624], P('attn', 'ffn')
The draws below stay inside these ranges and needn't reach their ends.
Inputs may be any that keep to these rules, and one draw needn't show every extreme that they name: `page_table`: entries past a request's length are unused; pages may be shared. `home_device`: among the 32 rows of one index of attn, at most 4 name the same attention device.
All inputs are finite; a program needn't handle non-finite values.
Results may differ from the reference program's by a relative error of at most 0.035.
Values may be sent and summed in bfloat16 or wider, within the bound.
No kernel may reach another device: no remote copies, remote signals or barrier semaphores. Data moves between devices by JAX's collectives and lax.ppermute only.
A program may use at most 128 MiB of HBM per device.

```python
import math
import jax
import jax.numpy as jnp
import numpy as np
from jax import lax

D = 16384
HEADS = 128
KV = 8
HD = 128
FF = 26624
PAGE = 16
CTX = 512
REQ_DEV = 32
POOL = 256
CAP = 4
MAXP = 32
REQS = 512
N_ATTN = 16


def draw_stream(key, part):
    key = jax.random.fold_in(key, 11)
    first, second, third = jax.random.split(key, 3)
    row_scale = jnp.exp(jax.random.uniform(second, (REQS, 1), jnp.float32, math.log(0.3), math.log(3.0)))
    column = jnp.arange(D, dtype=jnp.float32)[None, :] / D
    spread = (1.0 + 2.0 * column) * jnp.exp(jax.random.uniform(third, (1, D), jnp.float32, math.log(0.5), math.log(2.0)))
    values = 0.5 * jax.random.normal(first, (REQS, D), jnp.float32) * row_scale * spread
    return jnp.clip(values, -12.0, 12.0).astype(jnp.bfloat16)


def draw_queries(key, part):
    key = jax.random.fold_in(key, 23)
    third = jax.random.fold_in(key, 2)
    values = jax.random.normal(third, (REQS, HEADS, HD), jnp.float32)
    return jnp.clip(values, -16.0, 16.0).reshape(REQS, HEADS * HD).astype(jnp.bfloat16)


def draw_k_pool(key, part):
    key = jax.random.fold_in(key, 31)
    noise = jax.random.normal(key, (N_ATTN * POOL, PAGE, KV * HD), jnp.float32)
    values = noise
    return jnp.clip(values, -6.0, 6.0).astype(jnp.bfloat16)


def draw_lengths(key, part):
    key = jax.random.fold_in(key, 37)
    first, second = jax.random.split(key)
    values = jax.random.randint(first, (REQS,), 1, CTX + 1, jnp.int32)
    spot = jax.random.randint(second, (), 0, REQS, jnp.int32)
    return jnp.where(jnp.arange(REQS, dtype=jnp.int32) == spot, CTX, values).astype(jnp.int32)


def draw_page_table(key, part):
    key = jax.random.fold_in(key, 41)
    values = jax.random.randint(key, (REQS, MAXP), 0, POOL, jnp.int32)
    flat = jnp.arange(REQS * MAXP, dtype=jnp.int32).reshape(REQS, MAXP)
    values = jnp.where(flat == 0, POOL - 1, values)
    values = jnp.where(flat == 1, 0, values)
    return values.astype(jnp.int32)


def level_of(rng, extent, cuts, low, largest):
    loudness = 1.0
    for axis_at, blocks in cuts:
        heights = jax.random.uniform(jax.random.fold_in(jax.random.fold_in(rng, 6), axis_at), (blocks,), jnp.float32, low / len(cuts), largest / len(cuts))
        loudness = loudness * jnp.repeat(jnp.exp(heights), extent[axis_at] // blocks).reshape((-1,) + (1,) * (len(extent) - 1 - axis_at))
    return loudness


def routed_block(rng, own, number, rows, amount, top, limit, slope):
    order = jax.random.permutation(rng, amount)
    heavy_load, usual = shares(amount, rows * top, limit, slope, True), shares(amount, rows * top, limit, slope, False)
    places = jnp.arange(amount)

    def named(sizes, rotation):
        used = int((sizes > 0).sum())
        fixed = max(1, used // 4)
        moved = fixed + (places - fixed + rotation * (used - fixed)) % max(1, amount - fixed)
        return jnp.zeros((amount,), jnp.int32).at[order[jnp.where(places < fixed, places, moved)]].set(jnp.asarray(sizes, jnp.int32))

    sizes = jnp.where(number % 4 == 0, named(heavy_load, number // 4), named(usual, number - number // 4 - 1))
    mixed = jax.random.permutation(jax.random.fold_in(own, 3), amount)
    source_of, sink = mixed[0:amount // 2 * 2:2], mixed[1:amount // 2 * 2:2]
    slack = jnp.minimum(sizes[source_of] - 1, limit - sizes[sink]) // 2
    slack = jnp.where((source_of == order[0]) | (sink == order[0]) | (sizes[sink] == 0), 0, jnp.maximum(slack, 0))
    moved = jax.random.randint(jax.random.fold_in(own, 4), (amount // 2,), 0, 1 << 20) % (slack + 1)
    sizes = sizes.at[source_of].add(-moved).at[sink].add(moved)
    items = jnp.searchsorted(jnp.cumsum(sizes), jnp.arange(rows * top), side="right").astype(jnp.int32)
    listing = items.reshape(top, rows).T
    listing = listing[jax.random.permutation(jax.random.fold_in(own, 1), rows)]
    rotation = jax.random.randint(jax.random.fold_in(own, 2), (rows, 1), 0, top)
    return jnp.take_along_axis(listing, (jnp.arange(top)[None, :] + rotation) % top, axis=1)


def shares(amount, total, reach, skew, full):
    weights = [(1 << 20) // math.isqrt(standing ** skew) + 1 for standing in range(1, amount + 1)]
    largest = reach if full else min(reach, max(-(-total // amount), total * weights[0] // sum(weights)))
    least = 1 if total - largest >= amount - 1 else 0
    counts, spare = [largest] + [least] * (amount - 1), total - largest - least * (amount - 1)
    while spare > 0:
        free = [i for i in range(1, amount) if counts[i] < largest] or [i for i in range(1, amount) if counts[i] < reach]
        pool, left = sum([weights[i] for i in free]), spare
        for i in free:
            more = min(reach - counts[i], max(1, left * weights[i] // pool), spare)
            counts[i] = counts[i] + more
            spare = spare - more
    return np.array(counts)


def gaussian(own_key, shape, scale, most, cuts=(), kind=jnp.bfloat16):
    factor_of = level_of(own_key, shape, cuts, -0.22, 0.18) if cuts else 1.0
    array = jax.random.normal(own_key, shape, jnp.float32) * scale * factor_of
    return jnp.minimum(jnp.maximum(array, -most), most).astype(kind)


def setup_inputs(seed: int = 0) -> dict:
    arg_keys = jax.random.split(jax.random.key(seed), 12)
    stream = draw_stream(jax.random.fold_in(arg_keys[11], 71), 0)
    queries = draw_queries(jax.random.fold_in(arg_keys[11], 71), 0)
    k_pool = draw_k_pool(jax.random.fold_in(arg_keys[11], 71), 0)
    v_pool = gaussian(arg_keys[3], (N_ATTN * POOL, PAGE, KV * HD), 4.0, 24.0, ((0, 16), (2, 8)))
    page_table = draw_page_table(jax.random.fold_in(arg_keys[11], 71), 0)
    lengths = draw_lengths(jax.random.fold_in(arg_keys[11], 71), 0)
    home_device_keys = jax.random.split(jax.random.fold_in(arg_keys[6], 1), REQS // REQ_DEV)
    home_device_turns = jax.random.permutation(jax.random.fold_in(arg_keys[6], 3), REQS // REQ_DEV)
    home_device = jax.vmap(lambda own, number: routed_block(jax.random.fold_in(arg_keys[6], 2), own, number, REQ_DEV, N_ATTN, 1, CAP, 2))(home_device_keys, home_device_turns).reshape((REQS, 1))
    w_out = gaussian(arg_keys[7], (HEADS * HD, D), (HEADS * HD) ** -0.5, 0.046875, ((0, 8), (1, 16)))
    norm_gain = jnp.clip(1.0 + 0.18 * jax.random.normal(arg_keys[8], (D,), jnp.float32), 0.099609375, 1.8984375).astype(jnp.bfloat16)
    w_gate = gaussian(arg_keys[9], (D, FF), D ** -0.5, 0.046875, ((0, 16), (1, 8)))
    w_up = gaussian(arg_keys[10], (D, FF), D ** -0.5, 0.046875, ((0, 16), (1, 8)))
    return {"stream": stream, "queries": queries, "k_pool": k_pool, "v_pool": v_pool, "page_table": page_table, "lengths": lengths, "home_device": home_device, "w_out": w_out, "norm_gain": norm_gain, "w_gate": w_gate, "w_up": w_up}


eps = 1e-05

def reference(stream, queries, k_pool, v_pool, page_table, lengths, home_device, w_out, norm_gain, w_gate, w_up):
    pages = home_device[:, :1] * POOL + page_table
    per_group = HEADS // KV

    def attend_one(inputs):
        query_row, page_row, length = inputs
        key_rows = k_pool[page_row].reshape(CTX, KV, HD).astype(jnp.float32)
        value_rows = v_pool[page_row].reshape(CTX, KV, HD).astype(jnp.float32)
        queried = query_row.reshape(KV, per_group, HD).astype(jnp.float32)
        scores = jnp.einsum('kgd,tkd->kgt', queried, key_rows) * HD ** (-0.5)
        visible = (jnp.arange(CTX, dtype=jnp.int32) < length)[None, None, :]
        maxima = lax.optimization_barrier(jnp.max(jnp.where(visible, scores, -jnp.inf), axis=-1, keepdims=True))
        weights = jnp.where(visible, jnp.exp(scores - maxima), jnp.float32(0.0))
        totals = lax.optimization_barrier(jnp.sum(weights, axis=-1))
        rounded = weights.astype(jnp.bfloat16).astype(jnp.float32)
        blended = jnp.einsum('kgt,tkd->kgd', rounded, value_rows) / totals[..., None]
        return blended.astype(jnp.bfloat16).reshape(-1)
    attention = lax.map(attend_one, (queries, pages, lengths))
    attended = jnp.dot(attention, w_out, preferred_element_type=jnp.float32)
    residual = (stream.astype(jnp.float32) + attended).astype(jnp.bfloat16)
    widened = residual.astype(jnp.float32)
    scaling = lax.rsqrt(lax.optimization_barrier(jnp.mean(widened * widened, axis=1)) + eps)
    normed = (widened * scaling[:, None] * norm_gain.astype(jnp.float32)[None, :]).astype(jnp.bfloat16)
    width_block = D // N_ATTN

    def block_sum(carry, index):
        start = index * width_block
        rows = lax.dynamic_slice_in_dim(normed, start, width_block, 1)
        gate_part = jnp.dot(rows, lax.dynamic_slice_in_dim(w_gate, start, width_block, 0), preferred_element_type=jnp.float32)
        up_part = jnp.dot(rows, lax.dynamic_slice_in_dim(w_up, start, width_block, 0), preferred_element_type=jnp.float32)
        gate_low = lax.optimization_barrier(gate_part.astype(jnp.bfloat16))
        up_low = lax.optimization_barrier(up_part.astype(jnp.bfloat16))
        return ((carry[0] + gate_low.astype(jnp.float32), carry[1] + up_low.astype(jnp.float32)), None)
    start_sums = (jnp.zeros((REQS, FF), jnp.float32), jnp.zeros((REQS, FF), jnp.float32))
    (gate, up_sum), _ = lax.scan(block_sum, start_sums, jnp.arange(N_ATTN, dtype=jnp.int32))
    hidden = (jax.nn.silu(gate) * up_sum).astype(jnp.bfloat16)
    return (residual, hidden)
```

```python
import functools
import jax
import jax.numpy as jnp
from jax import lax
from jax.experimental import pallas as pl
from jax.experimental.pallas import tpu as pltpu
from jax.sharding import PartitionSpec as P

D = 16384
HD = 128
HEADS = 16
PAGE = 16
MAXP = 32
CTX = PAGE * MAXP
REQS = 512
N_ATTN = 16
ROWS = 32
CAP = 4
SLOTS = N_ATTN * CAP
SIDE = 4
WIDTH = 1024
GROUP = 4
EPS = 1e-05
VMEM_BYTES = 50 * 1024 * 1024

SMEM = pl.BlockSpec(memory_space=pltpu.SMEM)
VMEM = pl.BlockSpec(memory_space=pltpu.VMEM)


def params():
    return pltpu.CompilerParams(vmem_limit_bytes=VMEM_BYTES)


def dispatch_body(mine_ref, home_ref, queries_ref, out_ref, count_ref):
    out_ref[...] = jnp.zeros_like(out_ref)
    for target in range(N_ATTN):
        count_ref[target] = 0
    base = mine_ref[0] * ROWS
    for row in range(ROWS):
        target = home_ref[0, base + row]
        rank = count_ref[target]
        count_ref[target] = rank + 1
        out_ref[target * CAP + rank] = queries_ref[row]


def dispatch(mine, home, queries):
    return pl.pallas_call(
        dispatch_body,
        out_shape=jax.ShapeDtypeStruct((SLOTS, HEADS, HD), jnp.bfloat16),
        in_specs=[SMEM, SMEM, VMEM],
        out_specs=VMEM,
        scratch_shapes=[pltpu.SMEM((N_ATTN,), jnp.int32)],
        compiler_params=params(),
    )(mine, home, queries)


def attend_body(
    mine_ref,
    home_ref,
    lengths_ref,
    table_ref,
    queries_ref,
    k_ref,
    v_ref,
    out_ref,
    ids_ref,
    slots_ref,
):
    mine = mine_ref[0]
    out_ref[...] = jnp.zeros_like(out_ref)

    def scan_source(source, found):
        start = found
        for row in range(ROWS):
            request = source * ROWS + row
            ids_ref[found] = request
            slots_ref[found] = source * CAP + found - start
            found = found + jnp.where(home_ref[0, request] == mine, 1, 0)
        return found

    found = lax.fori_loop(0, N_ATTN, scan_source, jnp.int32(0))
    last = jnp.maximum(found - 1, 0)
    last_id = ids_ref[last]
    last_slot = slots_ref[last]
    for extra in range(GROUP):
        ids_ref[found + extra] = last_id
        slots_ref[found + extra] = last_slot

    positions = lax.broadcasted_iota(jnp.int32, (HEADS, CTX), 1)

    def step(index, carry):
        chosen = []
        for member in range(GROUP):
            place = index * GROUP + member
            request = ids_ref[place]
            slot = slots_ref[place]
            pages = [table_ref[page, request] for page in range(MAXP)]
            chosen.append((request, slot, pages))
        scores = []
        for request, slot, pages in chosen:
            keys = jnp.concatenate([k_ref[page] for page in pages], axis=0)
            scores.append(
                lax.dot_general(
                    queries_ref[slot],
                    keys,
                    (((1,), (1,)), ((), ())),
                    preferred_element_type=jnp.float32,
                )
                * HD ** (-0.5)
            )
        outputs = []
        for (request, slot, pages), score in zip(chosen, scores):
            visible = positions < lengths_ref[0, request]
            maxima = jnp.max(jnp.where(visible, score, -jnp.inf), axis=1, keepdims=True)
            weights = jnp.where(visible, jnp.exp(score - maxima), 0.0)
            totals = jnp.sum(weights, axis=1, keepdims=True)
            outputs.append((weights.astype(jnp.bfloat16), totals))
        for (request, slot, pages), (weights, totals) in zip(chosen, outputs):
            values = jnp.concatenate([v_ref[page] for page in pages], axis=0)
            blended = jnp.dot(weights, values, preferred_element_type=jnp.float32)
            out_ref[slot] = (blended / totals).astype(jnp.bfloat16)
        return carry

    lax.fori_loop(0, (found + GROUP - 1) // GROUP, step, 0)


def attend(mine, home, lengths, table, queries, k_pool, v_pool):
    return pl.pallas_call(
        attend_body,
        out_shape=jax.ShapeDtypeStruct((SLOTS, HEADS, HD), jnp.bfloat16),
        in_specs=[SMEM] * 4 + [VMEM] * 3,
        out_specs=VMEM,
        scratch_shapes=[
            pltpu.SMEM((SLOTS + GROUP + 4,), jnp.int32),
            pltpu.SMEM((SLOTS + GROUP + 4,), jnp.int32),
        ],
        compiler_params=params(),
    )(mine, home, lengths, table, queries, k_pool, v_pool)


def collect_body(mine_ref, home_ref, slots_ref, out_ref, wide_ref, count_ref):
    for target in range(N_ATTN):
        count_ref[target] = 0
    base = mine_ref[0] * ROWS
    for row in range(ROWS):
        target = home_ref[0, base + row]
        rank = count_ref[target]
        count_ref[target] = rank + 1
        heads = slots_ref[target * CAP + rank].astype(jnp.float32)
        for head in range(HEADS):
            wide_ref[row : row + 1, head * HD : (head + 1) * HD] = heads[head : head + 1]
    out_ref[...] = wide_ref[...].astype(jnp.bfloat16)


def collect(mine, home, slots):
    return pl.pallas_call(
        collect_body,
        out_shape=jax.ShapeDtypeStruct((ROWS, HEADS * HD), jnp.bfloat16),
        in_specs=[SMEM, SMEM, VMEM],
        out_specs=VMEM,
        scratch_shapes=[
            pltpu.VMEM((ROWS, HEADS * HD), jnp.float32),
            pltpu.SMEM((N_ATTN,), jnp.int32),
        ],
        compiler_params=params(),
    )(mine, home, slots)


TILE = 256


def project_body(count, picks_ref, rows_ref, weight_ref, out_ref):
    blocks = [rows_ref[picks_ref[2 * k], picks_ref[2 * k + 1]] for k in range(count)]
    lhs = jnp.concatenate(blocks, axis=0)
    out_ref[...] = jnp.dot(lhs, weight_ref[...], preferred_element_type=jnp.float32).astype(
        jnp.bfloat16
    )


def project(picks, rows, weight):
    count = picks.shape[0] // 2
    columns = weight.shape[1]
    return pl.pallas_call(
        functools.partial(project_body, count),
        out_shape=jax.ShapeDtypeStruct((count * ROWS, columns), jnp.bfloat16),
        grid_spec=pltpu.PrefetchScalarGridSpec(
            num_scalar_prefetch=1,
            grid=(columns // TILE,),
            in_specs=[
                pl.BlockSpec((SIDE, SIDE, ROWS, WIDTH), lambda n, _: (0, 0, 0, 0)),
                pl.BlockSpec((WIDTH, TILE), lambda n, _: (0, n)),
            ],
            out_specs=pl.BlockSpec((count * ROWS, TILE), lambda n, _: (0, n)),
        ),
        compiler_params=params(),
    )(picks, rows, weight)


def merge_body(picks_ref, own_ref, direct_ref, relayed_ref, one_ref, two_ref, three_ref, home_ref, sums_ref):
    sums_ref[...] = (
        own_ref[...].astype(jnp.float32)
        + direct_ref[...].astype(jnp.float32)
        + relayed_ref[...].astype(jnp.float32)
    )
    for k, out in enumerate((one_ref, two_ref, three_ref)):
        out[...] = sums_ref[picks_ref[k]].astype(jnp.bfloat16)
    home_ref[...] = sums_ref[picks_ref[3]]


def merge(picks, own, direct, relayed):
    columns = own.shape[-1]
    own, direct, relayed = (a.reshape(SIDE, ROWS, columns) for a in (own, direct, relayed))
    return pl.pallas_call(
        merge_body,
        out_shape=[jax.ShapeDtypeStruct((ROWS, columns), jnp.bfloat16)] * 3
        + [jax.ShapeDtypeStruct((ROWS, columns), jnp.float32)],
        in_specs=[SMEM] + [VMEM] * 3,
        out_specs=[VMEM] * 4,
        scratch_shapes=[pltpu.VMEM((SIDE, ROWS, columns), jnp.float32)],
        compiler_params=params(),
    )(picks, own, direct, relayed)


def along_z(x, shift):
    return lax.ppermute(
        x, "attn", [(y * SIDE + z, y * SIDE + (z + shift) % SIDE) for y in range(SIDE) for z in range(SIDE)]
    )


def along_y(x, shift):
    return lax.ppermute(
        x, "attn", [(y * SIDE + z, (y + shift) % SIDE * SIDE + z) for y in range(SIDE) for z in range(SIDE)]
    )


def to_sibling(x):
    return lax.ppermute(x, "ffn", [(f, f ^ 1) for f in range(8)])


def along_x(x):
    groups = [[chip * 2 + core for chip in range(SIDE)] for core in range(2)]
    return lax.all_to_all(x, "ffn", split_axis=0, concat_axis=0, axis_index_groups=groups, tiled=True)


def scatter_start(shift, pick, here, rows, weight):
    two, one, minus = (here + 2) % SIDE, (here + 1) % SIDE, (here + 3) % SIDE
    first = project(pick([(two, 0), (one, 1), (two, 1), (minus, 0)]), rows, weight)
    columns = weight.shape[1]
    first = first.reshape(2, 2 * SIDE * ROWS // 2, columns)
    up = shift(first[0], 1)
    down = shift(first[1], -1)
    return up, down


def scatter_finish(shift, cross, pick, here, there, up, down, rows, weight):
    columns = weight.shape[1]
    half = 2 * ROWS
    one, minus = (here + 1) % SIDE, (here + 3) % SIDE
    rest = project(pick([(one, 0), (minus, 1), (here, 0), (here, 1)]), rows, weight)
    f32 = jnp.float32
    up_next = (rest[:half].astype(f32) + up[:half].astype(f32)).astype(jnp.bfloat16)
    down_next = (rest[half : 2 * half].astype(f32) + down[:half].astype(f32)).astype(jnp.bfloat16)
    from_below = shift(up_next, 1)
    from_above = shift(down_next, -1)
    own = rest[2 * half :]
    direct = jnp.concatenate([down[half:], up[half:]], axis=0)
    relayed = jnp.concatenate([from_below, from_above], axis=0)
    picks = jnp.stack([(there + 1) % SIDE, (there + 2) % SIDE, (there + 3) % SIDE, there])
    one_on, two_on, three_on, mine = merge(picks, own, direct, relayed)
    return (mine, cross(one_on, 1), cross(two_on, 2), cross(three_on, 3))


def on_device(
    stream,
    queries,
    k_pool,
    v_pool,
    page_table,
    lengths,
    home_device,
    w_out,
    norm_gain,
    w_gate,
    w_up,
):
    f32 = jnp.float32
    attn = lax.axis_index("attn").astype(jnp.int32)
    ffn = lax.axis_index("ffn").astype(jnp.int32)
    chip, core = ffn // 2, ffn % 2
    y, z = attn // SIDE, attn % SIDE
    mine = attn.reshape(1)
    home = home_device.reshape(1, REQS)

    outgoing = dispatch(mine, home, queries.reshape(ROWS, HEADS, HD))
    arrived = lax.all_to_all(outgoing, "attn", split_axis=0, concat_axis=0, tiled=True)
    blended = attend(
        mine, home, lengths.reshape(1, REQS), page_table.T, arrived, k_pool, v_pool
    )
    returned = lax.all_to_all(blended, "attn", split_axis=0, concat_axis=0, tiled=True)
    attention = collect(mine, home, returned)
    gathered = lax.all_to_all(
        jnp.broadcast_to(attention[None], (N_ATTN,) + attention.shape),
        "attn",
        split_axis=0,
        concat_axis=0,
        tiled=True,
    ).reshape(REQS, HEADS * HD)
    partial = jnp.dot(gathered, w_out, preferred_element_type=f32).astype(jnp.bfloat16)

    half = REQS // 2
    part = half // SIDE
    kept = lax.dynamic_slice_in_dim(partial, core * half, half, 0)
    given = lax.dynamic_slice_in_dim(partial, (1 - core) * half, half, 0)
    pair = (kept.astype(f32) + to_sibling(given).astype(f32)).astype(jnp.bfloat16)
    pieces = along_x(pair.reshape(SIDE, part, WIDTH))
    stream_rows = lax.dynamic_slice_in_dim(stream, core * half + chip * part, part, 0)
    mine_rows = (stream_rows.astype(f32) + jnp.sum(pieces.astype(f32), axis=0)).astype(jnp.bfloat16)
    this_half = along_x(jnp.broadcast_to(mine_rows[None], (SIDE, part, WIDTH))).reshape(half, WIDTH)
    other_half = to_sibling(this_half)
    residual = jnp.where(
        core == 0,
        jnp.concatenate([this_half, other_half], axis=0),
        jnp.concatenate([other_half, this_half], axis=0),
    )
    widened = residual.astype(f32)
    squares = jnp.sum(widened * widened, axis=1)
    scaled = (widened * norm_gain.astype(f32)[None, :]).astype(jnp.bfloat16)
    rows = scaled.reshape(SIDE, SIDE, ROWS, WIDTH)

    def pick_z(pairs):
        return jnp.stack([i for at, h in pairs for k in (2 * h, 2 * h + 1) for i in (jnp.int32(k), at)])

    def pick_y(pairs):
        return jnp.stack([i for at, h in pairs for k in (2 * h, 2 * h + 1) for i in (at, jnp.int32(k))])

    square_sums = jnp.sum(
        lax.all_to_all(
            squares.reshape(N_ATTN, 1, ROWS), "attn", split_axis=0, concat_axis=0, tiled=True
        ),
        axis=(0, 1),
    )
    gate_up, gate_down = scatter_start(along_z, pick_z, z, rows, w_gate)
    up_up, up_down = scatter_start(along_y, pick_y, y, rows, w_up)
    gate_parts = scatter_finish(along_z, along_y, pick_z, z, y, gate_up, gate_down, rows, w_gate)
    up_parts = scatter_finish(along_y, along_z, pick_y, y, z, up_up, up_down, rows, w_up)
    scaling = lax.rsqrt(square_sums / D + EPS)[:, None]
    gate = sum(p.astype(f32) for p in gate_parts) * scaling
    up = sum(p.astype(f32) for p in up_parts) * scaling
    hidden = (jax.nn.silu(gate) * up).astype(jnp.bfloat16)
    return (residual, hidden)


def solution(mesh):
    return jax.shard_map(
        on_device,
        mesh=mesh,
        in_specs=(
            P(None, "attn"),
            P("attn", "ffn"),
            P("attn", None, "ffn"),
            P("attn", None, "ffn"),
            P(),
            P(),
            P(),
            P("ffn", "attn"),
            P("attn"),
            P("attn", "ffn"),
            P("attn", "ffn"),
        ),
        out_specs=(P(None, "attn"), P("attn", "ffn")),
        check_vma=False,
    )
```

```python
import functools
import jax
import jax.numpy as jnp
from jax import lax
from jax.experimental import pallas as pl
from jax.experimental.pallas import tpu as pltpu
from jax.sharding import PartitionSpec as P

D = 16384
HD = 128
HEADS = 16
PAGE = 16
MAXP = 32
CTX = PAGE * MAXP
REQS = 512
N_ATTN = 16
ROWS = 32
CAP = 4
SLOTS = N_ATTN * CAP
SIDE = 4
WIDTH = 1024
GROUP = 4
EPS = 1e-05

SMEM = pl.BlockSpec(memory_space=pltpu.SMEM)
VMEM = pl.BlockSpec(memory_space=pltpu.VMEM)
HBM = pl.BlockSpec(memory_space=pltpu.HBM)


WIDE = 58


def params(mebibytes=16):
    return pltpu.CompilerParams(vmem_limit_bytes=mebibytes * 1024 * 1024)


def start_all(copies):
    for copy in copies:
        copy.start()
    return copies


def dispatch_body(mine_ref, home_hbm, queries_hbm, out_ref, queries_ref, tall_ref, home_ref, count_ref, sems):
    pairs = ((home_hbm, home_ref), (queries_hbm, queries_ref))
    copies = start_all([pltpu.make_async_copy(a, b, sems.at[k]) for k, (a, b) in enumerate(pairs)])
    out_ref[...] = jnp.zeros_like(out_ref)
    for copy in copies:
        copy.wait()
    for head in range(HEADS):
        tall_ref[pl.ds(head, ROWS, stride=HEADS), :] = queries_ref[
            :, head * HD : (head + 1) * HD
        ].astype(jnp.float32)
    for target in range(N_ATTN):
        count_ref[target] = 0
    base = mine_ref[0] * ROWS
    for row in range(ROWS):
        target = home_ref[0, base + row]
        rank = count_ref[target]
        count_ref[target] = rank + 1
        out_ref[target * CAP + rank] = tall_ref[row * HEADS : (row + 1) * HEADS].astype(jnp.bfloat16)


def dispatch(mine, home, queries):
    return pl.pallas_call(
        dispatch_body,
        out_shape=jax.ShapeDtypeStruct((SLOTS, HEADS, HD), jnp.bfloat16),
        in_specs=[SMEM, HBM, HBM],
        out_specs=VMEM,
        scratch_shapes=[
            pltpu.VMEM((ROWS, HEADS * HD), jnp.bfloat16),
            pltpu.VMEM((ROWS * HEADS, HD), jnp.float32),
            pltpu.SMEM((1, REQS), jnp.int32),
            pltpu.SMEM((N_ATTN,), jnp.int32),
            pltpu.SemaphoreType.DMA((2,)),
        ],
        compiler_params=params(WIDE),
    )(mine, home, queries)


def attend_body(
    mine_ref,
    home_hbm,
    lengths_hbm,
    table_hbm,
    queries_ref,
    k_hbm,
    v_hbm,
    out_ref,
    home_ref,
    lengths_ref,
    table_ref,
    k_ref,
    v_ref,
    ids_ref,
    slots_ref,
    sems,
):
    pairs = (
        (home_hbm, home_ref),
        (lengths_hbm, lengths_ref),
        (table_hbm, table_ref),
        (k_hbm, k_ref),
        (v_hbm, v_ref),
    )
    copies = start_all([pltpu.make_async_copy(a, b, sems.at[k]) for k, (a, b) in enumerate(pairs)])
    mine = mine_ref[0]
    out_ref[...] = jnp.zeros_like(out_ref)
    copies[0].wait()

    def scan_source(source, found):
        start = found
        for row in range(ROWS):
            request = source * ROWS + row
            ids_ref[found] = request
            slots_ref[found] = source * CAP + found - start
            found = found + jnp.where(home_ref[0, request] == mine, 1, 0)
        return found

    found = lax.fori_loop(0, N_ATTN, scan_source, jnp.int32(0))
    last = jnp.maximum(found - 1, 0)
    last_id = ids_ref[last]
    last_slot = slots_ref[last]
    for extra in range(GROUP):
        ids_ref[found + extra] = last_id
        slots_ref[found + extra] = last_slot
    for copy in copies[1:]:
        copy.wait()

    positions = lax.broadcasted_iota(jnp.int32, (HEADS, CTX), 1)

    def step(index, carry):
        chosen = []
        for member in range(GROUP):
            place = index * GROUP + member
            request = ids_ref[place]
            slot = slots_ref[place]
            pages = [table_ref[page, request] for page in range(MAXP)]
            chosen.append((request, slot, pages))
        scores = []
        for request, slot, pages in chosen:
            keys = jnp.concatenate([k_ref[page] for page in pages], axis=0)
            scores.append(
                lax.dot_general(
                    queries_ref[slot],
                    keys,
                    (((1,), (1,)), ((), ())),
                    preferred_element_type=jnp.float32,
                )
                * HD ** (-0.5)
            )
        outputs = []
        for (request, slot, pages), score in zip(chosen, scores):
            visible = positions < lengths_ref[0, request]
            maxima = jnp.max(jnp.where(visible, score, -jnp.inf), axis=1, keepdims=True)
            weights = jnp.where(visible, jnp.exp(score - maxima), 0.0)
            totals = jnp.sum(weights, axis=1, keepdims=True)
            outputs.append((weights.astype(jnp.bfloat16), totals))
        for (request, slot, pages), (weights, totals) in zip(chosen, outputs):
            values = jnp.concatenate([v_ref[page] for page in pages], axis=0)
            blended = jnp.dot(weights, values, preferred_element_type=jnp.float32)
            out_ref[slot] = (blended / totals).astype(jnp.bfloat16)
        return carry

    lax.fori_loop(0, (found + GROUP - 1) // GROUP, step, 0)


def attend(mine, home, lengths, table, queries, k_pool, v_pool):
    return pl.pallas_call(
        attend_body,
        out_shape=jax.ShapeDtypeStruct((SLOTS, HEADS, HD), jnp.bfloat16),
        in_specs=[SMEM, HBM, HBM, HBM, VMEM, HBM, HBM],
        out_specs=VMEM,
        scratch_shapes=[
            pltpu.SMEM(home.shape, jnp.int32),
            pltpu.SMEM(lengths.shape, jnp.int32),
            pltpu.SMEM(table.shape, jnp.int32),
            pltpu.VMEM(k_pool.shape, jnp.bfloat16),
            pltpu.VMEM(v_pool.shape, jnp.bfloat16),
            pltpu.SMEM((SLOTS + GROUP + 4,), jnp.int32),
            pltpu.SMEM((SLOTS + GROUP + 4,), jnp.int32),
            pltpu.SemaphoreType.DMA((5,)),
        ],
        compiler_params=params(WIDE),
    )(mine, home, lengths, table, queries, k_pool, v_pool)


def collect_body(mine_ref, home_hbm, slots_ref, out_hbm, wide_ref, whole_ref, home_ref, count_ref, sem, sems):
    copy = pltpu.make_async_copy(home_hbm, home_ref, sem)
    copy.start()
    for target in range(N_ATTN):
        count_ref[target] = 0
    base = mine_ref[0] * ROWS
    copy.wait()
    for row in range(ROWS):
        target = home_ref[0, base + row]
        rank = count_ref[target]
        count_ref[target] = rank + 1
        heads = slots_ref[target * CAP + rank].astype(jnp.float32)
        for head in range(HEADS):
            wide_ref[row : row + 1, head * HD : (head + 1) * HD] = heads[head : head + 1]
    whole_ref[...] = wide_ref[...].astype(jnp.bfloat16)
    copies = start_all(
        [pltpu.make_async_copy(whole_ref, out_hbm.at[k], sems.at[k]) for k in range(N_ATTN)]
    )
    for copy in copies:
        copy.wait()


def collect(mine, home, slots):
    return pl.pallas_call(
        collect_body,
        out_shape=jax.ShapeDtypeStruct((N_ATTN, ROWS, HEADS * HD), jnp.bfloat16),
        in_specs=[SMEM, HBM, VMEM],
        out_specs=HBM,
        scratch_shapes=[
            pltpu.VMEM((ROWS, HEADS * HD), jnp.float32),
            pltpu.VMEM((ROWS, HEADS * HD), jnp.bfloat16),
            pltpu.SMEM((1, REQS), jnp.int32),
            pltpu.SMEM((N_ATTN,), jnp.int32),
            pltpu.SemaphoreType.DMA,
            pltpu.SemaphoreType.DMA((N_ATTN,)),
        ],
        compiler_params=params(),
    )(mine, home, slots)


def fetch_body(place_ref, out_hbm, gate_hbm, up_hbm, stream_hbm, gain_hbm, after_hbm, *refs):
    out_ref, gate_ref, up_ref, stream_ref, gain_ref, sems = refs
    part = stream_ref.shape[0]
    first = pl.multiple_of(place_ref[3] * (SIDE * part) + place_ref[2] * part, part)
    pairs = (
        (out_hbm, out_ref),
        (gate_hbm, gate_ref),
        (up_hbm, up_ref),
        (stream_hbm.at[pl.ds(first, part)], stream_ref),
        (gain_hbm, gain_ref),
    )
    copies = start_all([pltpu.make_async_copy(a, b, sems.at[k]) for k, (a, b) in enumerate(pairs)])
    for copy in copies:
        copy.wait()


def fetch(place, weights, stream, gain, after):
    shapes = [w.shape for w in weights] + [(REQS // 8, WIDTH), gain.shape]
    return pl.pallas_call(
        fetch_body,
        out_shape=[jax.ShapeDtypeStruct(shape, jnp.bfloat16) for shape in shapes],
        in_specs=[SMEM] + [HBM] * 6,
        out_specs=[VMEM] * 5,
        scratch_shapes=[pltpu.SemaphoreType.DMA((5,))],
        compiler_params=params(40),
    )(place, *weights, stream, gain, after)


def half_body(sibling, place_ref, rows_ref, weight_ref, out_ref):
    core = place_ref[3]
    which = 1 - core if sibling else core
    out_ref[...] = jnp.dot(
        rows_ref[which], weight_ref[...], preferred_element_type=jnp.float32
    ).astype(jnp.bfloat16)


def half_project(sibling, place, rows, weight):
    return pl.pallas_call(
        functools.partial(half_body, sibling),
        out_shape=jax.ShapeDtypeStruct((rows.shape[1], weight.shape[1]), jnp.bfloat16),
        in_specs=[SMEM, VMEM, VMEM],
        out_specs=VMEM,
        compiler_params=params(),
    )(place, rows, weight)


def relative(at):
    return [(at + 1) % SIDE, (at + 2) % SIDE, (at + 3) % SIDE, at]


def pair_body(place_ref, kept_ref, came_ref, one_ref, two_ref, three_ref, own_ref):
    for at, out in zip(relative(place_ref[2]), (one_ref, two_ref, three_ref, own_ref)):
        out[...] = (kept_ref[at].astype(jnp.float32) + came_ref[at].astype(jnp.float32)).astype(out.dtype)


def pair(place, kept, came):
    part = kept.shape[0] // SIDE
    shape = (part, WIDTH)
    return pl.pallas_call(
        pair_body,
        out_shape=[jax.ShapeDtypeStruct(shape, jnp.bfloat16)] * 3
        + [jax.ShapeDtypeStruct(shape, jnp.float32)],
        in_specs=[SMEM, VMEM, VMEM],
        out_specs=[VMEM] * 4,
        compiler_params=params(),
    )(place, kept.reshape(SIDE, part, WIDTH), came.reshape(SIDE, part, WIDTH))


def settle_body(stream_ref, own_ref, a_ref, b_ref, c_ref, out_ref):
    total = own_ref[...]
    for piece in (a_ref, b_ref, c_ref):
        total = total + piece[...].astype(jnp.float32)
    out_ref[...] = (stream_ref[...].astype(jnp.float32) + total).astype(jnp.bfloat16)


def settle(stream_rows, own, pieces):
    return pl.pallas_call(
        settle_body,
        out_shape=jax.ShapeDtypeStruct(own.shape, jnp.bfloat16),
        in_specs=[VMEM] * 5,
        out_specs=VMEM,
        compiler_params=params(),
    )(stream_rows, own, *pieces)


def lay_body(place_ref, one_ref, two_ref, three_ref, own_ref, out_ref):
    for at, block in zip(relative(place_ref[2]), (one_ref, two_ref, three_ref, own_ref)):
        out_ref[at] = block[...]


def lay(place, blocks):
    return pl.pallas_call(
        lay_body,
        out_shape=jax.ShapeDtypeStruct((SIDE,) + blocks[0].shape, jnp.bfloat16),
        in_specs=[SMEM] + [VMEM] * 4,
        out_specs=VMEM,
        compiler_params=params(),
    )(place, *blocks)


def assemble_body(place_ref, this_ref, other_ref, gain_ref, residual_ref, rows_ref, squares_ref):
    core = place_ref[3]
    gain = gain_ref[...].astype(jnp.float32)
    for which, half_ref in ((core, this_ref), (1 - core, other_ref)):
        size = half_ref.shape[0]
        residual_ref[pl.ds(pl.multiple_of(which * size, size), size), :] = half_ref[...]
        widened = half_ref[...].astype(jnp.float32)
        totals = jnp.sum(widened * widened, axis=1, keepdims=True)
        first = which * (SIDE // 2)
        rows_ref[pl.ds(first, SIDE // 2)] = (
            (widened * gain).astype(jnp.bfloat16).reshape(SIDE // 2, SIDE, ROWS, WIDTH)
        )
        squares_ref[pl.ds(first, SIDE // 2)] = jnp.broadcast_to(totals, (size, HD)).reshape(
            SIDE // 2, SIDE, ROWS, HD
        )


def assemble(place, this_half, other_half, gain):
    return pl.pallas_call(
        assemble_body,
        out_shape=[
            jax.ShapeDtypeStruct((REQS, WIDTH), jnp.bfloat16),
            jax.ShapeDtypeStruct((SIDE, SIDE, ROWS, WIDTH), jnp.bfloat16),
            jax.ShapeDtypeStruct((SIDE, SIDE, ROWS, HD), jnp.float32),
        ],
        in_specs=[SMEM] + [VMEM] * 3,
        out_specs=[VMEM] * 3,
        compiler_params=params(),
    )(place, this_half, other_half, gain)


def project_body(line, groups, came, squared, place_ref, rows_ref, weight_ref, *refs):
    refs = list(refs)
    squares_ref = refs.pop(0) if squared else None
    added = [refs.pop(0) for _ in range(came)]
    here = place_ref[line]
    at = []
    for step, half in groups:
        there = (here + step) % SIDE
        for other in (2 * half, 2 * half + 1):
            at.append((other, there) if line else (there, other))
    lhs = jnp.concatenate([rows_ref[i, j] for i, j in at], axis=0)
    columns = weight_ref.shape[1]
    size = 2 * ROWS
    product = jnp.dot(lhs, weight_ref[...], preferred_element_type=jnp.float32)
    for k, out in enumerate(refs):
        piece = product[size * k : size * (k + 1)]
        if k < came:
            piece = piece + added[k][:, :columns].astype(jnp.float32)
        out[:, :columns] = piece.astype(out.dtype)
        if squared:
            extra = jnp.concatenate([squares_ref[i, j] for i, j in at[2 * k : 2 * k + 2]], axis=0)
            if k < came:
                extra = extra + added[k][:, columns:].astype(jnp.float32)
            out[:, columns:] = extra.astype(out.dtype)


def project(line, groups, place, rows, weight, squares, dtypes, came=()):
    squared = squares is not None
    columns = weight.shape[1] + (HD if squared else 0)
    operands = [place, rows, weight] + ([squares] if squared else []) + list(came)
    return pl.pallas_call(
        functools.partial(project_body, line, groups, len(came), squared),
        out_shape=[jax.ShapeDtypeStruct((2 * ROWS, columns), dtype) for dtype in dtypes],
        in_specs=[SMEM] + [VMEM] * (len(operands) - 1),
        out_specs=[VMEM] * len(dtypes),
        compiler_params=params(),
    )(*operands)


def merge_body(line, place_ref, *refs):
    ins, (one_ref, two_ref, three_ref, home_ref, sums_ref) = refs[:6], refs[6:]
    for k in range(2):
        total = ins[k][...]
        for piece in (ins[2 + k], ins[4 + k]):
            total = total + piece[...].astype(jnp.float32)
        sums_ref[2 * k : 2 * k + 2] = total.reshape(2, ROWS, sums_ref.shape[2])
    for at, out in zip(relative(place_ref[line]), (one_ref, two_ref, three_ref, home_ref)):
        out[...] = sums_ref[at].astype(out.dtype)


def merge(line, place, own, direct, relayed):
    columns = own[0].shape[1]
    return pl.pallas_call(
        functools.partial(merge_body, line),
        out_shape=[jax.ShapeDtypeStruct((ROWS, columns), jnp.bfloat16)] * 3
        + [jax.ShapeDtypeStruct((ROWS, columns), jnp.float32)],
        in_specs=[SMEM] + [VMEM] * 6,
        out_specs=[VMEM] * 4,
        scratch_shapes=[pltpu.VMEM((SIDE, ROWS, columns), jnp.float32)],
        compiler_params=params(),
    )(place, *own, *direct, *relayed)


def along_z(x, shift):
    return lax.ppermute(
        x, "attn", [(y * SIDE + z, y * SIDE + (z + shift) % SIDE) for y in range(SIDE) for z in range(SIDE)]
    )


def along_y(x, shift):
    return lax.ppermute(
        x, "attn", [(y * SIDE + z, (y + shift) % SIDE * SIDE + z) for y in range(SIDE) for z in range(SIDE)]
    )


def along_x(x, shift):
    return lax.ppermute(
        x, "ffn", [(chip * 2 + core, (chip + shift) % SIDE * 2 + core) for chip in range(SIDE) for core in range(2)]
    )


def to_sibling(x):
    return lax.ppermute(x, "ffn", [(f, f ^ 1) for f in range(8)])


LINES = (along_y, along_z)


def scatter_far(line, place, rows, weight, squares):
    groups = ((2, 0), (2, 1))
    up, down = project(line, groups, place, rows, weight, squares, [jnp.bfloat16] * 2)
    return LINES[line](up, 1), LINES[line](down, 3)


def scatter_near(line, place, rows, weight, squares):
    groups = ((1, 1), (3, 0))
    up, down = project(line, groups, place, rows, weight, squares, [jnp.bfloat16] * 2)
    return LINES[line](down, 3), LINES[line](up, 1)


def scatter_relay(line, place, far, rows, weight, squares):
    groups = ((1, 0), (3, 1), (0, 0), (0, 1))
    dtypes = [jnp.bfloat16] * 2 + [jnp.float32] * 2
    up, down, first, second = project(line, groups, place, rows, weight, squares, dtypes, far)
    return (first, second), (LINES[line](up, 1), LINES[line](down, 3))


def scatter_cross(line, place, own, near, relayed):
    one, two, three, mine = merge(line, place, own, near, relayed)
    cross = LINES[line]
    return mine, cross(two, 2), cross(one, 1), cross(three, 3)


def on_device(
    stream,
    queries,
    k_pool,
    v_pool,
    page_table,
    lengths,
    home_device,
    w_out,
    norm_gain,
    w_gate,
    w_up,
):
    f32 = jnp.float32
    attn = lax.axis_index("attn").astype(jnp.int32)
    ffn = lax.axis_index("ffn").astype(jnp.int32)
    place = jnp.stack([attn // SIDE, attn % SIDE, ffn // 2, ffn % 2])
    mine = attn.reshape(1)
    home = home_device.reshape(1, REQS)

    outgoing = dispatch(mine, home, queries)
    arrived = lax.all_to_all(outgoing, "attn", split_axis=0, concat_axis=0, tiled=True)
    blended = attend(
        mine, home, lengths.reshape(1, REQS), page_table.T, arrived, k_pool, v_pool
    )
    returned = lax.all_to_all(blended, "attn", split_axis=0, concat_axis=0, tiled=True)
    copies = collect(mine, home, returned)
    half = REQS // 2
    out_weight, gate_weight, up_weight, stream_rows, gain = fetch(
        place, (w_out, w_gate, w_up), stream, norm_gain.reshape(1, WIDTH), copies
    )
    gathered = lax.all_to_all(copies, "attn", split_axis=0, concat_axis=0, tiled=True)
    gathered = gathered.reshape(2, half, HEADS * HD)

    came = to_sibling(half_project(True, place, gathered, out_weight))
    kept = half_project(False, place, gathered, out_weight)
    one, two, three, own = pair(place, kept, came)
    pieces = (along_x(two, 2), along_x(one, 1), along_x(three, 3))
    mine_rows = settle(stream_rows, own, pieces)
    others = (along_x(mine_rows, 3), along_x(mine_rows, 2), along_x(mine_rows, 1))
    this_half = lay(place, others + (mine_rows,)).reshape(half, WIDTH)
    other_half = to_sibling(this_half)
    residual, rows, squares = assemble(place, this_half, other_half, gain)

    gate_far = scatter_far(1, place, rows, gate_weight, squares)
    up_far = scatter_far(0, place, rows, up_weight, None)
    gate_near = scatter_near(1, place, rows, gate_weight, squares)
    up_near = scatter_near(0, place, rows, up_weight, None)
    gate_own, gate_relayed = scatter_relay(1, place, gate_far, rows, gate_weight, squares)
    up_own, up_relayed = scatter_relay(0, place, up_far, rows, up_weight, None)
    gate_parts = scatter_cross(0, place, gate_own, gate_near, gate_relayed)
    up_parts = scatter_cross(1, place, up_own, up_near, up_relayed)
    gate = sum(p.astype(f32) for p in gate_parts)
    columns = w_gate.shape[1]
    scaling = lax.rsqrt(gate[:, columns : columns + 1] / D + EPS)
    gate = gate[:, :columns] * scaling
    up = sum(p.astype(f32) for p in up_parts) * scaling
    hidden = (jax.nn.silu(gate) * up).astype(jnp.bfloat16)
    return (residual, hidden)


def solution(mesh):
    return jax.shard_map(
        on_device,
        mesh=mesh,
        in_specs=(
            P(None, "attn"),
            P("attn", "ffn"),
            P("attn", None, "ffn"),
            P("attn", None, "ffn"),
            P(),
            P(),
            P(),
            P("ffn", "attn"),
            P("attn"),
            P("attn", "ffn"),
            P("attn", "ffn"),
        ),
        out_specs=(P(None, "attn"), P("attn", "ffn")),
        check_vma=False,
    )
```

```python
import functools
import jax
import jax.numpy as jnp
from jax import lax
from jax.experimental import pallas as pl
from jax.experimental.pallas import tpu as pltpu
from jax.sharding import PartitionSpec as P

D = 16384
HD = 128
HEADS = 16
PAGE = 16
MAXP = 32
CTX = PAGE * MAXP
REQS = 512
N_ATTN = 16
ROWS = 32
CAP = 4
SLOTS = N_ATTN * CAP
SIDE = 4
WIDTH = 1024
GROUP = 8
LISTED = 128
SHORT = MAXP // 2
EPS = 1e-05

SMEM = pl.BlockSpec(memory_space=pltpu.SMEM)
VMEM = pl.BlockSpec(memory_space=pltpu.VMEM)
HBM = pl.BlockSpec(memory_space=pltpu.HBM)


WIDE = 58


def params(mebibytes=16):
    return pltpu.CompilerParams(vmem_limit_bytes=mebibytes * 1024 * 1024)


def place():
    attn, ffn = lax.axis_index("attn"), lax.axis_index("ffn")
    return attn // SIDE, attn % SIDE, ffn // 2, ffn % 2


def start_all(copies):
    for copy in copies:
        copy.start()
    return copies


def dispatch_body(home_hbm, queries_hbm, out_ref, dest_ref, queries_ref, tall_ref, home_ref, count_ref, sems):
    pairs = ((home_hbm, home_ref), (queries_hbm, queries_ref))
    copies = start_all([pltpu.make_async_copy(a, b, sems.at[k]) for k, (a, b) in enumerate(pairs)])
    out_ref[...] = jnp.zeros_like(out_ref)
    for target in range(N_ATTN):
        count_ref[target] = 0
    base = (lax.axis_index("attn")) * ROWS
    copies[0].wait()
    dests = []
    for row in range(ROWS):
        target = home_ref[0, base + row]
        rank = count_ref[target]
        count_ref[target] = rank + 1
        dests.append(target * CAP + rank)
        dest_ref[row] = dests[row]
    copies[1].wait()
    for head in range(HEADS):
        tall_ref[pl.ds(head, ROWS, stride=HEADS), :] = queries_ref[
            :, head * HD : (head + 1) * HD
        ].astype(jnp.float32)
    for row in range(ROWS):
        out_ref[dests[row]] = tall_ref[row * HEADS : (row + 1) * HEADS].astype(jnp.bfloat16)


def dispatch(home, queries):
    return pl.pallas_call(
        dispatch_body,
        out_shape=[
            jax.ShapeDtypeStruct((SLOTS, HEADS, HD), jnp.bfloat16),
            jax.ShapeDtypeStruct((ROWS,), jnp.int32),
        ],
        in_specs=[HBM, HBM],
        out_specs=[VMEM, SMEM],
        scratch_shapes=[
            pltpu.VMEM((ROWS, HEADS * HD), jnp.bfloat16),
            pltpu.VMEM((ROWS * HEADS, HD), jnp.float32),
            pltpu.SMEM((1, REQS), jnp.int32),
            pltpu.SMEM((N_ATTN,), jnp.int32),
            pltpu.SemaphoreType.DMA((2,)),
        ],
        compiler_params=params(WIDE),
    )(home, queries)


def prepare_body(home_hbm, *refs):
    sources, list_ref, targets = refs[:4], refs[4], refs[5:9]
    home_ref, lengths_ref, found_ref, sems = refs[9:]
    pairs = [(home_hbm, home_ref), (sources[0], lengths_ref)] + list(zip(sources, targets))
    copies = start_all([pltpu.make_async_copy(a, b, sems.at[k]) for k, (a, b) in enumerate(pairs)])
    mine = lax.axis_index("attn")
    copies[0].wait()

    def scan_source(source, found):
        for row in range(ROWS):
            request = source * ROWS + row
            found_ref[found] = request
            found = found + jnp.where(home_ref[0, request] == mine, 1, 0)
        return found

    total = lax.fori_loop(0, N_ATTN, scan_source, jnp.int32(0))
    copies[1].wait()

    def sort_entry(index, state):
        short, long, before, rank = state
        request = found_ref[index]
        source = request // ROWS
        rank = jnp.where(source == before, rank + 1, 0)
        entry = request * SLOTS + source * CAP + rank
        list_ref[0, short] = entry
        list_ref[1, long] = entry
        is_long = jnp.where(lengths_ref[0, request] > SHORT * PAGE, 1, 0)
        return short + 1 - is_long, long + is_long, source, rank

    zero = jnp.int32(0)
    counts = lax.fori_loop(0, total, sort_entry, (zero, zero, zero - 1, zero))[:2]
    for kind in range(2):
        last = list_ref[kind, jnp.maximum(counts[kind] - 1, 0)]
        for extra in range(GROUP):
            list_ref[kind, counts[kind] + extra] = last
        list_ref[kind, LISTED - 1] = counts[kind]
    for copy in copies[2:]:
        copy.wait()


def prepare(home, *arrays):
    return pl.pallas_call(
        prepare_body,
        out_shape=[jax.ShapeDtypeStruct((2, LISTED), jnp.int32)]
        + [jax.ShapeDtypeStruct(a.shape, a.dtype) for a in arrays],
        in_specs=[HBM] * 5,
        out_specs=[SMEM] + [VMEM] * 4,
        scratch_shapes=[
            pltpu.SMEM(home.shape, jnp.int32),
            pltpu.SMEM(arrays[0].shape, jnp.int32),
            pltpu.SMEM((LISTED,), jnp.int32),
            pltpu.SemaphoreType.DMA((6,)),
        ],
        compiler_params=params(),
    )(home, *arrays)


def attend_body(lengths_vmem, table_vmem, list_ref, queries_ref, k_ref, v_ref, out_ref, lengths_ref, table_ref, sems):
    pairs = ((lengths_vmem, lengths_ref), (table_vmem, table_ref))
    copies = start_all([pltpu.make_async_copy(a, b, sems.at[k]) for k, (a, b) in enumerate(pairs)])
    out_ref[...] = jnp.zeros_like(out_ref)
    for copy in copies:
        copy.wait()

    def step(kind, count, index, carry):
        positions = lax.broadcasted_iota(jnp.int32, (HEADS, count * PAGE), 1)
        chosen = []
        for member in range(GROUP):
            entry = list_ref[kind, index * GROUP + member]
            request, slot = entry // SLOTS, entry % SLOTS
            pages = [table_ref[page, request] for page in range(count)]
            chosen.append((request, slot, pages))
        scores = []
        for request, slot, pages in chosen:
            keys = jnp.concatenate([k_ref[page] for page in pages], axis=0)
            scores.append(
                lax.dot_general(
                    queries_ref[slot],
                    keys,
                    (((1,), (1,)), ((), ())),
                    preferred_element_type=jnp.float32,
                )
                * HD ** (-0.5)
            )
        outputs = []
        for (request, slot, pages), score in zip(chosen, scores):
            visible = positions < lengths_ref[0, request]
            maxima = jnp.max(jnp.where(visible, score, -jnp.inf), axis=1, keepdims=True)
            weights = jnp.where(visible, jnp.exp(score - maxima), 0.0)
            totals = jnp.sum(weights, axis=1, keepdims=True)
            outputs.append((weights.astype(jnp.bfloat16), totals))
        for (request, slot, pages), (weights, totals) in zip(chosen, outputs):
            values = jnp.concatenate([v_ref[page] for page in pages], axis=0)
            blended = jnp.dot(weights, values, preferred_element_type=jnp.float32)
            out_ref[slot] = (blended / totals).astype(jnp.bfloat16)
        return carry

    for kind, count in ((0, SHORT), (1, MAXP)):
        groups = (list_ref[kind, LISTED - 1] + GROUP - 1) // GROUP
        lax.fori_loop(0, groups, functools.partial(step, kind, count), 0)


def attend(listed, queries, lengths, table, k_pool, v_pool):
    return pl.pallas_call(
        attend_body,
        out_shape=jax.ShapeDtypeStruct((SLOTS, HEADS, HD), jnp.bfloat16),
        in_specs=[VMEM, VMEM, SMEM] + [VMEM] * 3,
        out_specs=VMEM,
        scratch_shapes=[
            pltpu.SMEM(lengths.shape, jnp.int32),
            pltpu.SMEM(table.shape, jnp.int32),
            pltpu.SemaphoreType.DMA((2,)),
        ],
        compiler_params=params(),
    )(lengths, table, listed, queries, k_pool, v_pool)


def collect_body(dest_ref, slots_ref, left_ref, right_ref, wide_ref):
    for row in range(ROWS):
        heads = slots_ref[dest_ref[row]].astype(jnp.float32)
        for head in range(HEADS):
            wide_ref[row : row + 1, head * HD : (head + 1) * HD] = heads[head : head + 1]
    left_ref[...] = wide_ref[:, :WIDTH].astype(jnp.bfloat16)
    right_ref[...] = wide_ref[:, WIDTH:].astype(jnp.bfloat16)


def collect(dest, slots):
    return pl.pallas_call(
        collect_body,
        out_shape=[jax.ShapeDtypeStruct((ROWS, WIDTH), jnp.bfloat16)] * 2,
        in_specs=[SMEM, VMEM],
        out_specs=[VMEM] * 2,
        scratch_shapes=[pltpu.VMEM((ROWS, HEADS * HD), jnp.float32)],
        compiler_params=params(),
    )(dest, slots)


def gather_line_body(*refs):
    for line, ins, out in ((1, refs[:4], refs[8]), (0, refs[4:8], refs[9])):
        for at, block in zip(relative(place()[line]), ins):
            out[at] = block[...]


def gather_line(left, right):
    return pl.pallas_call(
        gather_line_body,
        out_shape=[jax.ShapeDtypeStruct((SIDE, ROWS, WIDTH), jnp.bfloat16)] * 2,
        in_specs=[VMEM] * 8,
        out_specs=[VMEM] * 2,
        compiler_params=params(),
    )(*left, *right)


def gather_all_body(*refs):
    out = refs[8]
    for at, block in zip(relative(place()[0]), refs[:4]):
        out[pl.ds(at * SIDE, SIDE), :, :WIDTH] = block[...]
    for at, block in zip(relative(place()[1]), refs[4:8]):
        for y in range(SIDE):
            out[y * SIDE + at, :, WIDTH:] = block[y]


def gather_all(left, right):
    return pl.pallas_call(
        gather_all_body,
        out_shape=jax.ShapeDtypeStruct((N_ATTN, ROWS, HEADS * HD), jnp.bfloat16),
        in_specs=[VMEM] * 8,
        out_specs=VMEM,
        compiler_params=params(),
    )(*left, *right)


def own_stream_body(stream_hbm, after_hbm, out_ref, sem):
    part = out_ref.shape[0]
    first = pl.multiple_of(place()[3] * (SIDE * part) + place()[2] * part, part)
    pltpu.async_copy(stream_hbm.at[pl.ds(first, part)], out_ref, sem).wait()


def own_stream(stream, after):
    return pl.pallas_call(
        own_stream_body,
        out_shape=jax.ShapeDtypeStruct((REQS // 8, WIDTH), stream.dtype),
        in_specs=[HBM] * 2,
        out_specs=VMEM,
        scratch_shapes=[pltpu.SemaphoreType.DMA],
        compiler_params=params(),
    )(stream, after)


def half_body(sibling, rows_ref, weight_ref, out_ref):
    core = place()[3]
    which = 1 - core if sibling else core
    out_ref[...] = jnp.dot(
        rows_ref[which], weight_ref[...], preferred_element_type=jnp.float32
    ).astype(jnp.bfloat16)


def half_project(sibling, rows, weight):
    return pl.pallas_call(
        functools.partial(half_body, sibling),
        out_shape=jax.ShapeDtypeStruct((rows.shape[1], weight.shape[1]), jnp.bfloat16),
        in_specs=[VMEM, VMEM],
        out_specs=VMEM,
        compiler_params=params(),
    )(rows, weight)


def relative(at):
    return [(at + 1) % SIDE, (at + 2) % SIDE, (at + 3) % SIDE, at]


def pair_body(kept_ref, came_ref, one_ref, two_ref, three_ref, own_ref):
    for at, out in zip(relative(place()[2]), (one_ref, two_ref, three_ref, own_ref)):
        out[...] = (kept_ref[at].astype(jnp.float32) + came_ref[at].astype(jnp.float32)).astype(out.dtype)


def pair(kept, came):
    part = kept.shape[0] // SIDE
    shape = (part, WIDTH)
    return pl.pallas_call(
        pair_body,
        out_shape=[jax.ShapeDtypeStruct(shape, jnp.bfloat16)] * 3
        + [jax.ShapeDtypeStruct(shape, jnp.float32)],
        in_specs=[VMEM, VMEM],
        out_specs=[VMEM] * 4,
        compiler_params=params(),
    )(kept.reshape(SIDE, part, WIDTH), came.reshape(SIDE, part, WIDTH))


def settle_body(stream_ref, own_ref, a_ref, b_ref, c_ref, out_ref):
    total = own_ref[...]
    for piece in (a_ref, b_ref, c_ref):
        total = total + piece[...].astype(jnp.float32)
    out_ref[...] = (stream_ref[...].astype(jnp.float32) + total).astype(jnp.bfloat16)


def settle(stream_rows, own, pieces):
    return pl.pallas_call(
        settle_body,
        out_shape=jax.ShapeDtypeStruct(own.shape, jnp.bfloat16),
        in_specs=[VMEM] * 5,
        out_specs=VMEM,
        compiler_params=params(),
    )(stream_rows, own, *pieces)


def lay_body(one_ref, two_ref, three_ref, own_ref, out_ref):
    for at, block in zip(relative(place()[2]), (one_ref, two_ref, three_ref, own_ref)):
        out_ref[at] = block[...]


def lay(blocks):
    return pl.pallas_call(
        lay_body,
        out_shape=jax.ShapeDtypeStruct((SIDE,) + blocks[0].shape, jnp.bfloat16),
        in_specs=[VMEM] * 4,
        out_specs=VMEM,
        compiler_params=params(),
    )(*blocks)


def assemble_body(this_ref, other_ref, gain_ref, residual_ref, rows_ref, squares_ref):
    core = place()[3]
    gain = gain_ref[...].astype(jnp.float32)
    for which, half_ref in ((core, this_ref), (1 - core, other_ref)):
        size = half_ref.shape[0]
        residual_ref[pl.ds(pl.multiple_of(which * size, size), size), :] = half_ref[...]
        widened = half_ref[...].astype(jnp.float32)
        totals = jnp.sum(widened * widened, axis=1, keepdims=True)
        first = which * (SIDE // 2)
        rows_ref[pl.ds(first, SIDE // 2)] = (
            (widened * gain).astype(jnp.bfloat16).reshape(SIDE // 2, SIDE, ROWS, WIDTH)
        )
        squares_ref[pl.ds(first, SIDE // 2)] = jnp.broadcast_to(totals, (size, HD)).reshape(
            SIDE // 2, SIDE, ROWS, HD
        )


def assemble(this_half, other_half, gain):
    return pl.pallas_call(
        assemble_body,
        out_shape=[
            jax.ShapeDtypeStruct((REQS, WIDTH), jnp.bfloat16),
            jax.ShapeDtypeStruct((SIDE, SIDE, ROWS, WIDTH), jnp.bfloat16),
            jax.ShapeDtypeStruct((SIDE, SIDE, ROWS, HD), jnp.float32),
        ],
        in_specs=[VMEM] * 3,
        out_specs=[VMEM] * 3,
        compiler_params=params(),
    )(this_half, other_half, gain)


def project_body(lines, outs, came, rows_ref, squares_ref, *refs):
    refs = list(refs)
    weights = [refs.pop(0) for _ in lines]
    added = [[refs.pop(0) for _ in range(came)] for _ in lines]
    size = 2 * ROWS
    for line, weight_ref, pieces in zip(lines, weights, added):
        targets = []
        for k, groups in enumerate(outs):
            out = refs.pop(0)
            for first, group in enumerate(groups):
                targets.append((out, first * size, pieces[k] if k < came and first == 0 else None, group))
        here = place()[line]
        at = []
        for _, _, _, (step, half) in targets:
            there = (here + step) % SIDE
            for other in (2 * half, 2 * half + 1):
                at.append((other, there) if line else (there, other))
        lhs = jnp.concatenate([rows_ref[i, j] for i, j in at], axis=0)
        columns = weight_ref.shape[1]
        product = jnp.dot(lhs, weight_ref[...], preferred_element_type=jnp.float32)
        for k, (out, first, extra, _) in enumerate(targets):
            piece = product[size * k : size * (k + 1)]
            if extra is not None:
                piece = piece + extra[:, :columns].astype(jnp.float32)
            out[first : first + size, :columns] = piece.astype(out.dtype)
            if line:
                piece = jnp.concatenate([squares_ref[i, j] for i, j in at[2 * k : 2 * k + 2]], axis=0)
                if extra is not None:
                    piece = piece + extra[:, columns:].astype(jnp.float32)
                out[first : first + size, columns:] = piece.astype(out.dtype)


def project(lines, outs, rows, squares, weights, dtypes, came=()):
    columns = [weights[line].shape[1] + (HD if line else 0) for line in lines]
    operands = [rows, squares] + [weights[line] for line in lines]
    operands += [piece for line in lines for piece in (came[line] if came else ())]
    results = pl.pallas_call(
        functools.partial(project_body, lines, outs, 2 if came else 0),
        out_shape=[
            jax.ShapeDtypeStruct((2 * ROWS * len(groups), n), dtype)
            for n in columns
            for groups, dtype in zip(outs, dtypes)
        ],
        in_specs=[VMEM] * len(operands),
        out_specs=[VMEM] * (len(lines) * len(outs)),
        compiler_params=params(),
    )(*operands)
    size = len(outs)
    return {line: results[size * k : size * (k + 1)] for k, line in enumerate(lines)}


def merge_body(*refs):
    sums = refs[-2:]
    size = 2 * ROWS
    for line in range(2):
        own_ref, before_ref, after_ref = refs[3 * line : 3 * line + 3]
        outs = refs[6 + 4 * line : 10 + 4 * line]
        sums_ref = sums[line]
        for k in range(2):
            total = own_ref[size * k : size * (k + 1)]
            for ref, first in ((before_ref, size * k), (after_ref, size * (1 - k))):
                total = total + ref[first : first + size].astype(jnp.float32)
            sums_ref[2 * k : 2 * k + 2] = total.reshape(2, ROWS, sums_ref.shape[2])
        for at, out in zip(relative(place()[1 - line]), outs):
            out[...] = sums_ref[at].astype(out.dtype)


def merge(parts):
    columns = [parts[line][0].shape[1] for line in range(2)]
    results = pl.pallas_call(
        merge_body,
        out_shape=[
            jax.ShapeDtypeStruct((ROWS, n), dtype)
            for n in columns
            for dtype in [jnp.bfloat16] * 3 + [jnp.float32]
        ],
        in_specs=[VMEM] * 6,
        out_specs=[VMEM] * 8,
        scratch_shapes=[pltpu.VMEM((SIDE, ROWS, n), jnp.float32) for n in columns],
        compiler_params=params(),
    )(*parts[0], *parts[1])
    return results[:4], results[4:]


def along_z(x, shift):
    return lax.ppermute(
        x, "attn", [(y * SIDE + z, y * SIDE + (z + shift) % SIDE) for y in range(SIDE) for z in range(SIDE)]
    )


def along_y(x, shift):
    return lax.ppermute(
        x, "attn", [(y * SIDE + z, (y + shift) % SIDE * SIDE + z) for y in range(SIDE) for z in range(SIDE)]
    )


def along_x(x, shift):
    return lax.ppermute(
        x, "ffn", [(chip * 2 + core, (chip + shift) % SIDE * 2 + core) for chip in range(SIDE) for core in range(2)]
    )


def to_sibling(x):
    return lax.ppermute(x, "ffn", [(f, f ^ 1) for f in range(8)])


LINES = (along_y, along_z)


def scatter(rows, squares, weights):
    far = project((1, 0), (((2, 0),), ((2, 1),)), rows, squares, weights, [jnp.bfloat16] * 2)
    came = {line: (LINES[line](far[line][0], 1), LINES[line](far[line][1], 3)) for line in (1, 0)}
    parts = {}
    for line in (1, 0):
        outs = (((1, 0), (1, 1)), ((3, 1), (3, 0)), ((0, 0), (0, 1)))
        dtypes = [jnp.bfloat16, jnp.bfloat16, jnp.float32]
        up, down, own = project((line,), outs, rows, squares, weights, dtypes, came)[line]
        parts[line] = (own, LINES[line](up, 1), LINES[line](down, 3))
    up_blocks, gate_blocks = merge(parts)
    sums = []
    for cross, (one, two, three, mine) in ((along_y, gate_blocks), (along_z, up_blocks)):
        sums.append((mine, cross(two, 2), cross(one, 1), cross(three, 3)))
    return sums


def line_of(shift, x):
    two, one, three = shift(x, 2), shift(x, 3), shift(x, 1)
    return one, two, three, x


def on_device(
    stream,
    queries,
    k_pool,
    v_pool,
    page_table,
    lengths,
    home_device,
    w_out,
    norm_gain,
    w_gate,
    w_up,
):
    f32 = jnp.float32
    home = home_device.reshape(1, REQS)
    lengths = lengths.reshape(1, REQS)

    table = page_table.T
    outgoing, dest = dispatch(home, queries)
    listed, *here = prepare(home, lengths, table, k_pool, v_pool)
    arrived = lax.all_to_all(outgoing, "attn", split_axis=0, concat_axis=0, tiled=True)
    blended = attend(listed, arrived, *here)
    returned = lax.all_to_all(blended, "attn", split_axis=0, concat_axis=0, tiled=True)
    left, right = collect(dest, returned)
    stream_rows = own_stream(stream, left)
    left, right = gather_line(line_of(along_z, left), line_of(along_y, right))
    gathered = gather_all(line_of(along_y, left), line_of(along_z, right))
    half = REQS // 2
    gathered = gathered.reshape(2, half, HEADS * HD)

    came = to_sibling(half_project(True, gathered, w_out))
    kept = half_project(False, gathered, w_out)
    one, two, three, own = pair(kept, came)
    pieces = (along_x(two, 2), along_x(one, 1), along_x(three, 3))
    mine_rows = settle(stream_rows, own, pieces)
    others = (along_x(mine_rows, 3), along_x(mine_rows, 2), along_x(mine_rows, 1))
    this_half = lay(others + (mine_rows,)).reshape(half, WIDTH)
    other_half = to_sibling(this_half)
    residual, rows, squares = assemble(this_half, other_half, norm_gain.reshape(1, WIDTH))

    gate_parts, up_parts = scatter(rows, squares, (w_up, w_gate))
    gate = sum(p.astype(f32) for p in gate_parts)
    columns = w_gate.shape[1]
    scaling = lax.rsqrt(gate[:, columns : columns + 1] / D + EPS)
    gate = gate[:, :columns] * scaling
    up = sum(p.astype(f32) for p in up_parts) * scaling
    hidden = (jax.nn.silu(gate) * up).astype(jnp.bfloat16)
    return (residual, hidden)


def solution(mesh):
    return jax.shard_map(
        on_device,
        mesh=mesh,
        in_specs=(
            P(None, "attn"),
            P("attn", "ffn"),
            P("attn", None, "ffn"),
            P("attn", None, "ffn"),
            P(),
            P(),
            P(),
            P("ffn", "attn"),
            P("attn"),
            P("attn", "ffn"),
            P("attn", "ffn"),
        ),
        out_specs=(P(None, "attn"), P("attn", "ffn")),
        check_vma=False,
    )
```

```python
import functools
import jax
import jax.numpy as jnp
from jax import lax
from jax.experimental import pallas as pl
from jax.experimental.pallas import tpu as pltpu
from jax.sharding import PartitionSpec as P

D = 16384
HD = 128
HEADS = 16
PAGE = 16
MAXP = 32
CTX = PAGE * MAXP
REQS = 512
N_ATTN = 16
ROWS = 32
CAP = 4
SLOTS = N_ATTN * CAP
SIDE = 4
WIDTH = 1024
GROUP = 4
LISTED = 128
SHORT = MAXP // 2
EPS = 1e-05

SMEM = pl.BlockSpec(memory_space=pltpu.SMEM)
VMEM = pl.BlockSpec(memory_space=pltpu.VMEM)
HBM = pl.BlockSpec(memory_space=pltpu.HBM)


WIDE = 58


def params(mebibytes=16):
    return pltpu.CompilerParams(vmem_limit_bytes=mebibytes * 1024 * 1024)


def place():
    attn, ffn = lax.axis_index("attn"), lax.axis_index("ffn")
    return attn // SIDE, attn % SIDE, ffn // 2, ffn % 2


def start_all(copies):
    for copy in copies:
        copy.start()
    return copies


def dispatch_body(home_hbm, queries_hbm, out_ref, dest_ref, queries_ref, tall_ref, home_ref, count_ref, sems):
    pairs = ((home_hbm, home_ref), (queries_hbm, queries_ref))
    copies = start_all([pltpu.make_async_copy(a, b, sems.at[k]) for k, (a, b) in enumerate(pairs)])
    out_ref[...] = jnp.zeros_like(out_ref)
    for target in range(N_ATTN):
        count_ref[target] = 0
    base = (lax.axis_index("attn")) * ROWS
    copies[0].wait()
    dests = []
    for row in range(ROWS):
        target = home_ref[0, base + row]
        rank = count_ref[target]
        count_ref[target] = rank + 1
        dests.append(target * CAP + rank)
        dest_ref[row] = dests[row]
    copies[1].wait()
    for head in range(HEADS):
        tall_ref[pl.ds(head, ROWS, stride=HEADS), :] = queries_ref[
            :, head * HD : (head + 1) * HD
        ].astype(jnp.float32)
    for row in range(ROWS):
        out_ref[dests[row]] = tall_ref[row * HEADS : (row + 1) * HEADS].astype(jnp.bfloat16)


def dispatch(home, queries):
    return pl.pallas_call(
        dispatch_body,
        out_shape=[
            jax.ShapeDtypeStruct((SLOTS, HEADS, HD), jnp.bfloat16),
            jax.ShapeDtypeStruct((ROWS,), jnp.int32),
        ],
        in_specs=[HBM, HBM],
        out_specs=[VMEM, SMEM],
        scratch_shapes=[
            pltpu.VMEM((ROWS, HEADS * HD), jnp.bfloat16),
            pltpu.VMEM((ROWS * HEADS, HD), jnp.float32),
            pltpu.SMEM((1, REQS), jnp.int32),
            pltpu.SMEM((N_ATTN,), jnp.int32),
            pltpu.SemaphoreType.DMA((2,)),
        ],
        compiler_params=params(WIDE),
    )(home, queries)


def prepare_body(home_hbm, *refs):
    sources, list_ref, targets = refs[:4], refs[4], refs[5:9]
    home_ref, lengths_ref, found_ref, sems = refs[9:]
    pairs = [(home_hbm, home_ref), (sources[0], lengths_ref)] + list(zip(sources, targets))
    copies = start_all([pltpu.make_async_copy(a, b, sems.at[k]) for k, (a, b) in enumerate(pairs)])
    mine = lax.axis_index("attn")
    copies[0].wait()

    def scan_source(source, found):
        for row in range(ROWS):
            request = source * ROWS + row
            found_ref[found] = request
            found = found + jnp.where(home_ref[0, request] == mine, 1, 0)
        return found

    total = lax.fori_loop(0, N_ATTN, scan_source, jnp.int32(0))
    copies[1].wait()

    def sort_entry(index, state):
        short, long, before, rank = state
        request = found_ref[index]
        source = request // ROWS
        rank = jnp.where(source == before, rank + 1, 0)
        entry = request * SLOTS + source * CAP + rank
        list_ref[0, short] = entry
        list_ref[1, long] = entry
        is_long = jnp.where(lengths_ref[0, request] > SHORT * PAGE, 1, 0)
        return short + 1 - is_long, long + is_long, source, rank

    zero = jnp.int32(0)
    counts = lax.fori_loop(0, total, sort_entry, (zero, zero, zero - 1, zero))[:2]
    for kind in range(2):
        last = list_ref[kind, jnp.maximum(counts[kind] - 1, 0)]
        for extra in range(GROUP):
            list_ref[kind, counts[kind] + extra] = last
        list_ref[kind, LISTED - 1] = counts[kind]
    for copy in copies[2:]:
        copy.wait()


def prepare(home, *arrays):
    return pl.pallas_call(
        prepare_body,
        out_shape=[jax.ShapeDtypeStruct((2, LISTED), jnp.int32)]
        + [jax.ShapeDtypeStruct(a.shape, a.dtype) for a in arrays],
        in_specs=[HBM] * 5,
        out_specs=[SMEM] + [VMEM] * 4,
        scratch_shapes=[
            pltpu.SMEM(home.shape, jnp.int32),
            pltpu.SMEM(arrays[0].shape, jnp.int32),
            pltpu.SMEM((LISTED,), jnp.int32),
            pltpu.SemaphoreType.DMA((6,)),
        ],
        compiler_params=params(),
    )(home, *arrays)


def attend_body(lengths_vmem, table_vmem, list_ref, queries_ref, k_ref, v_ref, out_ref, lengths_ref, table_ref, sems):
    first, rest = pl.ds(0, SHORT), pl.ds(SHORT, MAXP - SHORT)
    pairs = (
        (lengths_vmem, lengths_ref),
        (table_vmem.at[first], table_ref.at[first]),
        (table_vmem.at[rest], table_ref.at[rest]),
    )
    copies = start_all([pltpu.make_async_copy(a, b, sems.at[k]) for k, (a, b) in enumerate(pairs)])
    out_ref[...] = jnp.zeros_like(out_ref)
    copies[0].wait()
    copies[1].wait()

    def step(kind, count, index, carry):
        positions = lax.broadcasted_iota(jnp.int32, (HEADS, count * PAGE), 1)
        chosen = []
        for member in range(GROUP):
            entry = list_ref[kind, index * GROUP + member]
            request, slot = entry // SLOTS, entry % SLOTS
            pages = [table_ref[page, request] for page in range(count)]
            chosen.append((request, slot, pages))
        scores = []
        for request, slot, pages in chosen:
            keys = jnp.concatenate([k_ref[page] for page in pages], axis=0)
            scores.append(
                lax.dot_general(
                    queries_ref[slot],
                    keys,
                    (((1,), (1,)), ((), ())),
                    preferred_element_type=jnp.float32,
                )
                * HD ** (-0.5)
            )
        outputs = []
        for (request, slot, pages), score in zip(chosen, scores):
            visible = positions < lengths_ref[0, request]
            maxima = jnp.max(jnp.where(visible, score, -jnp.inf), axis=1, keepdims=True)
            weights = jnp.where(visible, jnp.exp(score - maxima), 0.0)
            totals = jnp.sum(weights, axis=1, keepdims=True)
            outputs.append((weights.astype(jnp.bfloat16), totals))
        for (request, slot, pages), (weights, totals) in zip(chosen, outputs):
            values = jnp.concatenate([v_ref[page] for page in pages], axis=0)
            blended = jnp.dot(weights, values, preferred_element_type=jnp.float32)
            out_ref[slot] = (blended / totals).astype(jnp.bfloat16)
        return carry

    for kind, count in ((0, SHORT), (1, MAXP)):
        if kind:
            copies[2].wait()
        groups = (list_ref[kind, LISTED - 1] + GROUP - 1) // GROUP
        lax.fori_loop(0, groups, functools.partial(step, kind, count), 0)


def attend(listed, queries, lengths, table, k_pool, v_pool):
    return pl.pallas_call(
        attend_body,
        out_shape=jax.ShapeDtypeStruct((SLOTS, HEADS, HD), jnp.bfloat16),
        in_specs=[VMEM, VMEM, SMEM] + [VMEM] * 3,
        out_specs=VMEM,
        scratch_shapes=[
            pltpu.SMEM(lengths.shape, jnp.int32),
            pltpu.SMEM(table.shape, jnp.int32),
            pltpu.SemaphoreType.DMA((3,)),
        ],
        compiler_params=params(),
    )(lengths, table, listed, queries, k_pool, v_pool)


def collect_body(dest_ref, slots_ref, left_ref, right_ref, wide_ref):
    for row in range(ROWS):
        heads = slots_ref[dest_ref[row]].astype(jnp.float32)
        for head in range(HEADS):
            wide_ref[row : row + 1, head * HD : (head + 1) * HD] = heads[head : head + 1]
    left_ref[...] = wide_ref[:, :WIDTH].astype(jnp.bfloat16)
    right_ref[...] = wide_ref[:, WIDTH:].astype(jnp.bfloat16)


def collect(dest, slots):
    return pl.pallas_call(
        collect_body,
        out_shape=[jax.ShapeDtypeStruct((ROWS, WIDTH), jnp.bfloat16)] * 2,
        in_specs=[SMEM, VMEM],
        out_specs=[VMEM] * 2,
        scratch_shapes=[pltpu.VMEM((ROWS, HEADS * HD), jnp.float32)],
        compiler_params=params(),
    )(dest, slots)


def gather_line_body(*refs):
    for line, ins, out in ((1, refs[:4], refs[8]), (0, refs[4:8], refs[9])):
        for at, block in zip(relative(place()[line]), ins):
            out[at] = block[...]


def gather_line(left, right):
    return pl.pallas_call(
        gather_line_body,
        out_shape=[jax.ShapeDtypeStruct((SIDE, ROWS, WIDTH), jnp.bfloat16)] * 2,
        in_specs=[VMEM] * 8,
        out_specs=[VMEM] * 2,
        compiler_params=params(),
    )(*left, *right)


def gather_all_body(*refs):
    out = refs[8]
    for at, block in zip(relative(place()[0]), refs[:4]):
        out[pl.ds(at * SIDE, SIDE), :, :WIDTH] = block[...]
    for at, block in zip(relative(place()[1]), refs[4:8]):
        for y in range(SIDE):
            out[y * SIDE + at, :, WIDTH:] = block[y]


def gather_all(left, right):
    return pl.pallas_call(
        gather_all_body,
        out_shape=jax.ShapeDtypeStruct((N_ATTN, ROWS, HEADS * HD), jnp.bfloat16),
        in_specs=[VMEM] * 8,
        out_specs=VMEM,
        compiler_params=params(),
    )(*left, *right)


def own_stream_body(stream_hbm, after_hbm, out_ref, sem):
    part = out_ref.shape[0]
    first = pl.multiple_of(place()[3] * (SIDE * part) + place()[2] * part, part)
    pltpu.async_copy(stream_hbm.at[pl.ds(first, part)], out_ref, sem).wait()


def own_stream(stream, after):
    return pl.pallas_call(
        own_stream_body,
        out_shape=jax.ShapeDtypeStruct((REQS // 8, WIDTH), stream.dtype),
        in_specs=[HBM] * 2,
        out_specs=VMEM,
        scratch_shapes=[pltpu.SemaphoreType.DMA],
        compiler_params=params(),
    )(stream, after)


def half_body(sibling, rows_ref, weight_ref, out_ref):
    core = place()[3]
    which = 1 - core if sibling else core
    out_ref[...] = jnp.dot(
        rows_ref[which], weight_ref[...], preferred_element_type=jnp.float32
    ).astype(jnp.bfloat16)


def half_project(sibling, rows, weight):
    return pl.pallas_call(
        functools.partial(half_body, sibling),
        out_shape=jax.ShapeDtypeStruct((rows.shape[1], weight.shape[1]), jnp.bfloat16),
        in_specs=[VMEM, VMEM],
        out_specs=VMEM,
        compiler_params=params(),
    )(rows, weight)


def relative(at):
    return [(at + 1) % SIDE, (at + 2) % SIDE, (at + 3) % SIDE, at]


def pair_body(kept_ref, came_ref, one_ref, two_ref, three_ref, own_ref):
    for at, out in zip(relative(place()[2]), (one_ref, two_ref, three_ref, own_ref)):
        out[...] = (kept_ref[at].astype(jnp.float32) + came_ref[at].astype(jnp.float32)).astype(out.dtype)


def pair(kept, came):
    part = kept.shape[0] // SIDE
    shape = (part, WIDTH)
    return pl.pallas_call(
        pair_body,
        out_shape=[jax.ShapeDtypeStruct(shape, jnp.bfloat16)] * 3
        + [jax.ShapeDtypeStruct(shape, jnp.float32)],
        in_specs=[VMEM, VMEM],
        out_specs=[VMEM] * 4,
        compiler_params=params(),
    )(kept.reshape(SIDE, part, WIDTH), came.reshape(SIDE, part, WIDTH))


def settle_body(stream_ref, own_ref, a_ref, b_ref, c_ref, out_ref):
    total = own_ref[...]
    for piece in (a_ref, b_ref, c_ref):
        total = total + piece[...].astype(jnp.float32)
    out_ref[...] = (stream_ref[...].astype(jnp.float32) + total).astype(jnp.bfloat16)


def settle(stream_rows, own, pieces):
    return pl.pallas_call(
        settle_body,
        out_shape=jax.ShapeDtypeStruct(own.shape, jnp.bfloat16),
        in_specs=[VMEM] * 5,
        out_specs=VMEM,
        compiler_params=params(),
    )(stream_rows, own, *pieces)


def lay_body(one_ref, two_ref, three_ref, own_ref, out_ref):
    for at, block in zip(relative(place()[2]), (one_ref, two_ref, three_ref, own_ref)):
        out_ref[at] = block[...]


def lay(blocks):
    return pl.pallas_call(
        lay_body,
        out_shape=jax.ShapeDtypeStruct((SIDE,) + blocks[0].shape, jnp.bfloat16),
        in_specs=[VMEM] * 4,
        out_specs=VMEM,
        compiler_params=params(),
    )(*blocks)


def assemble_body(this_ref, other_ref, gain_ref, residual_ref, rows_ref, squares_ref):
    core = place()[3]
    gain = gain_ref[...].astype(jnp.float32)
    for which, half_ref in ((core, this_ref), (1 - core, other_ref)):
        size = half_ref.shape[0]
        residual_ref[pl.ds(pl.multiple_of(which * size, size), size), :] = half_ref[...]
        widened = half_ref[...].astype(jnp.float32)
        totals = jnp.sum(widened * widened, axis=1, keepdims=True)
        first = which * (SIDE // 2)
        rows_ref[pl.ds(first, SIDE // 2)] = (
            (widened * gain).astype(jnp.bfloat16).reshape(SIDE // 2, SIDE, ROWS, WIDTH)
        )
        squares_ref[pl.ds(first, SIDE // 2)] = jnp.broadcast_to(totals, (size, HD)).reshape(
            SIDE // 2, SIDE, ROWS, HD
        )


def assemble(this_half, other_half, gain):
    return pl.pallas_call(
        assemble_body,
        out_shape=[
            jax.ShapeDtypeStruct((REQS, WIDTH), jnp.bfloat16),
            jax.ShapeDtypeStruct((SIDE, SIDE, ROWS, WIDTH), jnp.bfloat16),
            jax.ShapeDtypeStruct((SIDE, SIDE, ROWS, HD), jnp.float32),
        ],
        in_specs=[VMEM] * 3,
        out_specs=[VMEM] * 3,
        compiler_params=params(),
    )(this_half, other_half, gain)


def project_body(outs, rows_ref, squares_ref, *refs):
    size = 2 * ROWS
    for line in (1, 0):
        weight_ref = refs[line]
        here = place()[line]
        targets, at = [], []
        for k, groups in enumerate(outs):
            out = refs[2 + line * len(outs) + k]
            for first, (step, half) in enumerate(groups):
                targets.append((out, first * size))
                there = (here + step) % SIDE
                for other in (2 * half, 2 * half + 1):
                    at.append((other, there) if line else (there, other))
        lhs = jnp.concatenate([rows_ref[i, j] for i, j in at], axis=0)
        columns = weight_ref.shape[1]
        product = jnp.dot(lhs, weight_ref[...], preferred_element_type=jnp.float32)
        for k, (out, first) in enumerate(targets):
            out[first : first + size, :columns] = product[size * k : size * (k + 1)].astype(out.dtype)
            if line:
                piece = jnp.concatenate([squares_ref[i, j] for i, j in at[2 * k : 2 * k + 2]], axis=0)
                out[first : first + size, columns:] = piece.astype(out.dtype)


def project(outs, rows, squares, weights, dtypes):
    columns = [weights[0].shape[1], weights[1].shape[1] + HD]
    results = pl.pallas_call(
        functools.partial(project_body, outs),
        out_shape=[
            jax.ShapeDtypeStruct((2 * ROWS * len(groups), n), dtype)
            for n in columns
            for groups, dtype in zip(outs, dtypes)
        ],
        in_specs=[VMEM] * 4,
        out_specs=[VMEM] * (2 * len(outs)),
        compiler_params=params(24),
    )(rows, squares, *weights)
    return results[: len(outs)], results[len(outs) :]


def relay_body(*refs):
    size = 2 * ROWS
    for k in range(2):
        part_ref, near_ref, came_ref, out = refs[k], refs[2 + k], refs[4 + k], refs[6 + k]
        out[:size] = (part_ref[...] + came_ref[...].astype(jnp.float32)).astype(out.dtype)
        out[size:] = near_ref[...]


def relay(parts, nears, came):
    shape = (4 * ROWS, parts[0].shape[1])
    return pl.pallas_call(
        relay_body,
        out_shape=[jax.ShapeDtypeStruct(shape, jnp.bfloat16)] * 2,
        in_specs=[VMEM] * 6,
        out_specs=[VMEM] * 2,
        compiler_params=params(),
    )(*parts, *nears, *came)


def merge_body(line, own_ref, before_ref, after_ref, *refs):
    outs, sums_ref = refs[:4], refs[4]
    size = 2 * ROWS
    for k in range(2):
        total = own_ref[size * k : size * (k + 1)]
        for ref, first in ((before_ref, size * k), (after_ref, size * (1 - k))):
            total = total + ref[first : first + size].astype(jnp.float32)
        sums_ref[2 * k : 2 * k + 2] = total.reshape(2, ROWS, sums_ref.shape[2])
    for at, out in zip(relative(place()[1 - line]), outs):
        out[...] = sums_ref[at].astype(out.dtype)


def merge(line, own, before, after):
    columns = own.shape[1]
    return pl.pallas_call(
        functools.partial(merge_body, line),
        out_shape=[jax.ShapeDtypeStruct((ROWS, columns), jnp.bfloat16)] * 3
        + [jax.ShapeDtypeStruct((ROWS, columns), jnp.float32)],
        in_specs=[VMEM] * 3,
        out_specs=[VMEM] * 4,
        scratch_shapes=[pltpu.VMEM((SIDE, ROWS, columns), jnp.float32)],
        compiler_params=params(),
    )(own, before, after)


def along_z(x, shift):
    return lax.ppermute(
        x, "attn", [(y * SIDE + z, y * SIDE + (z + shift) % SIDE) for y in range(SIDE) for z in range(SIDE)]
    )


def along_y(x, shift):
    return lax.ppermute(
        x, "attn", [(y * SIDE + z, (y + shift) % SIDE * SIDE + z) for y in range(SIDE) for z in range(SIDE)]
    )


def along_x(x, shift):
    return lax.ppermute(
        x, "ffn", [(chip * 2 + core, (chip + shift) % SIDE * 2 + core) for chip in range(SIDE) for core in range(2)]
    )


def to_sibling(x):
    return lax.ppermute(x, "ffn", [(f, f ^ 1) for f in range(8)])


LINES = (along_y, along_z)


def scatter(rows, squares, weights):
    far = project((((2, 0),), ((2, 1),)), rows, squares, weights, [jnp.bfloat16] * 2)
    came = {line: (LINES[line](far[line][0], 1), LINES[line](far[line][1], 3)) for line in (1, 0)}
    outs = (((1, 0),), ((3, 1),), ((1, 1),), ((3, 0),), ((0, 0), (0, 1)))
    dtypes = [jnp.float32] * 2 + [jnp.bfloat16] * 2 + [jnp.float32]
    rest = project(outs, rows, squares, weights, dtypes)
    parts = {}
    for line in (1, 0):
        up, down = relay(rest[line][:2], rest[line][2:4], came[line])
        parts[line] = (rest[line][4], LINES[line](up, 1), LINES[line](down, 3))
    sums = []
    for line in (1, 0):
        cross = LINES[1 - line]
        one, two, three, mine = merge(line, *parts[line])
        sums.append((mine, cross(two, 2), cross(one, 1), cross(three, 3)))
    return sums


def line_of(shift, x):
    two, one, three = shift(x, 2), shift(x, 3), shift(x, 1)
    return one, two, three, x


def on_device(
    stream,
    queries,
    k_pool,
    v_pool,
    page_table,
    lengths,
    home_device,
    w_out,
    norm_gain,
    w_gate,
    w_up,
):
    f32 = jnp.float32
    home = home_device.reshape(1, REQS)
    lengths = lengths.reshape(1, REQS)

    table = page_table.T
    outgoing, dest = dispatch(home, queries)
    listed, *here = prepare(home, lengths, table, k_pool, v_pool)
    arrived = lax.all_to_all(outgoing, "attn", split_axis=0, concat_axis=0, tiled=True)
    blended = attend(listed, arrived, *here)
    returned = lax.all_to_all(blended, "attn", split_axis=0, concat_axis=0, tiled=True)
    left, right = collect(dest, returned)
    stream_rows = own_stream(stream, left)
    left, right = gather_line(line_of(along_z, left), line_of(along_y, right))
    gathered = gather_all(line_of(along_y, left), line_of(along_z, right))
    half = REQS // 2
    gathered = gathered.reshape(2, half, HEADS * HD)

    came = to_sibling(half_project(True, gathered, w_out))
    kept = half_project(False, gathered, w_out)
    one, two, three, own = pair(kept, came)
    pieces = (along_x(two, 2), along_x(one, 1), along_x(three, 3))
    mine_rows = settle(stream_rows, own, pieces)
    others = (along_x(mine_rows, 3), along_x(mine_rows, 2), along_x(mine_rows, 1))
    this_half = lay(others + (mine_rows,)).reshape(half, WIDTH)
    other_half = to_sibling(this_half)
    residual, rows, squares = assemble(this_half, other_half, norm_gain.reshape(1, WIDTH))

    gate_parts, up_parts = scatter(rows, squares, (w_up, w_gate))
    gate = sum(p.astype(f32) for p in gate_parts)
    columns = w_gate.shape[1]
    scaling = lax.rsqrt(gate[:, columns : columns + 1] / D + EPS)
    gate = gate[:, :columns] * scaling
    up = sum(p.astype(f32) for p in up_parts) * scaling
    hidden = (jax.nn.silu(gate) * up).astype(jnp.bfloat16)
    return (residual, hidden)


def solution(mesh):
    return jax.shard_map(
        on_device,
        mesh=mesh,
        in_specs=(
            P(None, "attn"),
            P("attn", "ffn"),
            P("attn", None, "ffn"),
            P("attn", None, "ffn"),
            P(),
            P(),
            P(),
            P("ffn", "attn"),
            P("attn"),
            P("attn", "ffn"),
            P("attn", "ffn"),
        ),
        out_specs=(P(None, "attn"), P("attn", "ffn")),
        check_vma=False,
    )
```

```python
import functools
import jax
import jax.numpy as jnp
from jax import lax
from jax.experimental import pallas as pl
from jax.experimental.pallas import tpu as pltpu
from jax.sharding import PartitionSpec as P

D = 16384
HD = 128
HEADS = 16
PAGE = 16
MAXP = 32
CTX = PAGE * MAXP
REQS = 512
N_ATTN = 16
ROWS = 32
CAP = 4
SLOTS = N_ATTN * CAP
SIDE = 4
WIDTH = 1024
GROUP = 8
LISTED = 128
SHORT = MAXP // 2
EPS = 1e-05

SMEM = pl.BlockSpec(memory_space=pltpu.SMEM)
VMEM = pl.BlockSpec(memory_space=pltpu.VMEM)
HBM = pl.BlockSpec(memory_space=pltpu.HBM)


WIDE = 58


def params(mebibytes=16):
    return pltpu.CompilerParams(vmem_limit_bytes=mebibytes * 1024 * 1024)


def place():
    attn, ffn = lax.axis_index("attn"), lax.axis_index("ffn")
    return attn // SIDE, attn % SIDE, ffn // 2, ffn % 2


def start_all(copies):
    for copy in copies:
        copy.start()
    return copies


def dispatch_body(home_hbm, queries_hbm, out_ref, dest_ref, queries_ref, tall_ref, home_ref, count_ref, sems):
    pairs = ((home_hbm, home_ref), (queries_hbm, queries_ref))
    copies = start_all([pltpu.make_async_copy(a, b, sems.at[k]) for k, (a, b) in enumerate(pairs)])
    out_ref[...] = jnp.zeros_like(out_ref)
    for target in range(N_ATTN):
        count_ref[target] = 0
    base = (lax.axis_index("attn")) * ROWS
    copies[0].wait()
    dests = []
    for row in range(ROWS):
        target = home_ref[0, base + row]
        rank = count_ref[target]
        count_ref[target] = rank + 1
        dests.append(target * CAP + rank)
        dest_ref[row] = dests[row]
    copies[1].wait()
    for head in range(HEADS):
        tall_ref[pl.ds(head, ROWS, stride=HEADS), :] = queries_ref[
            :, head * HD : (head + 1) * HD
        ].astype(jnp.float32)
    for row in range(ROWS):
        out_ref[dests[row]] = tall_ref[row * HEADS : (row + 1) * HEADS].astype(jnp.bfloat16)


def dispatch(home, queries):
    return pl.pallas_call(
        dispatch_body,
        out_shape=[
            jax.ShapeDtypeStruct((SLOTS, HEADS, HD), jnp.bfloat16),
            jax.ShapeDtypeStruct((ROWS,), jnp.int32),
        ],
        in_specs=[HBM, HBM],
        out_specs=[VMEM, SMEM],
        scratch_shapes=[
            pltpu.VMEM((ROWS, HEADS * HD), jnp.bfloat16),
            pltpu.VMEM((ROWS * HEADS, HD), jnp.float32),
            pltpu.SMEM((1, REQS), jnp.int32),
            pltpu.SMEM((N_ATTN,), jnp.int32),
            pltpu.SemaphoreType.DMA((2,)),
        ],
        compiler_params=params(WIDE),
    )(home, queries)


def prepare_body(home_hbm, *refs):
    sources, list_ref, targets = refs[:4], refs[4], refs[5:9]
    home_ref, lengths_ref, found_ref, sems = refs[9:]
    pairs = [(home_hbm, home_ref), (sources[0], lengths_ref)] + list(zip(sources, targets))
    copies = start_all([pltpu.make_async_copy(a, b, sems.at[k]) for k, (a, b) in enumerate(pairs)])
    mine = lax.axis_index("attn")
    copies[0].wait()

    def scan_source(source, found):
        for row in range(ROWS):
            request = source * ROWS + row
            found_ref[found] = request
            found = found + jnp.where(home_ref[0, request] == mine, 1, 0)
        return found

    total = lax.fori_loop(0, N_ATTN, scan_source, jnp.int32(0))
    copies[1].wait()

    def sort_entry(index, state):
        short, long, before, rank = state
        request = found_ref[index]
        source = request // ROWS
        rank = jnp.where(source == before, rank + 1, 0)
        entry = request * SLOTS + source * CAP + rank
        list_ref[0, short] = entry
        list_ref[1, long] = entry
        is_long = jnp.where(lengths_ref[0, request] > SHORT * PAGE, 1, 0)
        return short + 1 - is_long, long + is_long, source, rank

    zero = jnp.int32(0)
    counts = lax.fori_loop(0, total, sort_entry, (zero, zero, zero - 1, zero))[:2]
    for kind in range(2):
        last = list_ref[kind, jnp.maximum(counts[kind] - 1, 0)]
        for extra in range(GROUP):
            list_ref[kind, counts[kind] + extra] = last
        list_ref[kind, LISTED - 1] = counts[kind]
    for copy in copies[2:]:
        copy.wait()


def prepare(home, *arrays):
    return pl.pallas_call(
        prepare_body,
        out_shape=[jax.ShapeDtypeStruct((2, LISTED), jnp.int32)]
        + [jax.ShapeDtypeStruct(a.shape, a.dtype) for a in arrays],
        in_specs=[HBM] * 5,
        out_specs=[SMEM] + [VMEM] * 4,
        scratch_shapes=[
            pltpu.SMEM(home.shape, jnp.int32),
            pltpu.SMEM(arrays[0].shape, jnp.int32),
            pltpu.SMEM((LISTED,), jnp.int32),
            pltpu.SemaphoreType.DMA((6,)),
        ],
        compiler_params=params(),
    )(home, *arrays)


def attend_body(lengths_vmem, table_vmem, list_ref, queries_ref, k_ref, v_ref, out_ref, lengths_ref, table_ref, sems):
    first, rest = pl.ds(0, SHORT), pl.ds(SHORT, MAXP - SHORT)
    pairs = (
        (lengths_vmem, lengths_ref),
        (table_vmem.at[first], table_ref.at[first]),
        (table_vmem.at[rest], table_ref.at[rest]),
    )
    copies = start_all([pltpu.make_async_copy(a, b, sems.at[k]) for k, (a, b) in enumerate(pairs)])
    out_ref[...] = jnp.zeros_like(out_ref)
    copies[0].wait()
    copies[1].wait()

    def step(kind, count, index, carry):
        positions = lax.broadcasted_iota(jnp.int32, (HEADS, count * PAGE), 1)
        chosen = []
        for member in range(GROUP):
            entry = list_ref[kind, index * GROUP + member]
            request, slot = entry // SLOTS, entry % SLOTS
            pages = [table_ref[page, request] for page in range(count)]
            chosen.append((request, slot, pages))
        scores = []
        for request, slot, pages in chosen:
            keys = jnp.concatenate([k_ref[page] for page in pages], axis=0)
            scores.append(
                lax.dot_general(
                    queries_ref[slot],
                    keys,
                    (((1,), (1,)), ((), ())),
                    preferred_element_type=jnp.float32,
                )
                * HD ** (-0.5)
            )
        outputs = []
        for (request, slot, pages), score in zip(chosen, scores):
            visible = positions < lengths_ref[0, request]
            maxima = jnp.max(jnp.where(visible, score, -jnp.inf), axis=1, keepdims=True)
            weights = jnp.where(visible, jnp.exp(score - maxima), 0.0)
            totals = jnp.sum(weights, axis=1, keepdims=True)
            outputs.append((weights.astype(jnp.bfloat16), totals))
        for (request, slot, pages), (weights, totals) in zip(chosen, outputs):
            values = jnp.concatenate([v_ref[page] for page in pages], axis=0)
            blended = jnp.dot(weights, values, preferred_element_type=jnp.float32)
            out_ref[slot] = (blended / totals).astype(jnp.bfloat16)
        return carry

    for kind, count in ((0, SHORT), (1, MAXP)):
        if kind:
            copies[2].wait()
        groups = (list_ref[kind, LISTED - 1] + GROUP - 1) // GROUP
        lax.fori_loop(0, groups, functools.partial(step, kind, count), 0)


def attend(listed, queries, lengths, table, k_pool, v_pool):
    return pl.pallas_call(
        attend_body,
        out_shape=jax.ShapeDtypeStruct((SLOTS, HEADS, HD), jnp.bfloat16),
        in_specs=[VMEM, VMEM, SMEM] + [VMEM] * 3,
        out_specs=VMEM,
        scratch_shapes=[
            pltpu.SMEM(lengths.shape, jnp.int32),
            pltpu.SMEM(table.shape, jnp.int32),
            pltpu.SemaphoreType.DMA((3,)),
        ],
        compiler_params=params(),
    )(lengths, table, listed, queries, k_pool, v_pool)


def collect_body(dest_ref, slots_ref, left_ref, right_ref, wide_ref):
    for row in range(ROWS):
        heads = slots_ref[dest_ref[row]].astype(jnp.float32)
        for head in range(HEADS):
            wide_ref[row : row + 1, head * HD : (head + 1) * HD] = heads[head : head + 1]
    left_ref[...] = wide_ref[:, :WIDTH].astype(jnp.bfloat16)
    right_ref[...] = wide_ref[:, WIDTH:].astype(jnp.bfloat16)


def collect(dest, slots):
    return pl.pallas_call(
        collect_body,
        out_shape=[jax.ShapeDtypeStruct((ROWS, WIDTH), jnp.bfloat16)] * 2,
        in_specs=[SMEM, VMEM],
        out_specs=[VMEM] * 2,
        scratch_shapes=[pltpu.VMEM((ROWS, HEADS * HD), jnp.float32)],
        compiler_params=params(),
    )(dest, slots)


def gather_line_body(*refs):
    for line, ins, out in ((1, refs[:4], refs[8]), (0, refs[4:8], refs[9])):
        for at, block in zip(relative(place()[line]), ins):
            out[at] = block[...]


def gather_line(left, right):
    return pl.pallas_call(
        gather_line_body,
        out_shape=[jax.ShapeDtypeStruct((SIDE, ROWS, WIDTH), jnp.bfloat16)] * 2,
        in_specs=[VMEM] * 8,
        out_specs=[VMEM] * 2,
        compiler_params=params(),
    )(*left, *right)


def gather_all_body(*refs):
    out = refs[8]
    for at, block in zip(relative(place()[0]), refs[:4]):
        out[pl.ds(at * SIDE, SIDE), :, :WIDTH] = block[...]
    for at, block in zip(relative(place()[1]), refs[4:8]):
        for y in range(SIDE):
            out[y * SIDE + at, :, WIDTH:] = block[y]


def gather_all(left, right):
    return pl.pallas_call(
        gather_all_body,
        out_shape=jax.ShapeDtypeStruct((N_ATTN, ROWS, HEADS * HD), jnp.bfloat16),
        in_specs=[VMEM] * 8,
        out_specs=VMEM,
        compiler_params=params(),
    )(*left, *right)


def own_stream_body(stream_hbm, after_hbm, out_ref, sem):
    part = out_ref.shape[0]
    first = pl.multiple_of(place()[3] * (SIDE * part) + place()[2] * part, part)
    pltpu.async_copy(stream_hbm.at[pl.ds(first, part)], out_ref, sem).wait()


def own_stream(stream, after):
    return pl.pallas_call(
        own_stream_body,
        out_shape=jax.ShapeDtypeStruct((REQS // 8, WIDTH), stream.dtype),
        in_specs=[HBM] * 2,
        out_specs=VMEM,
        scratch_shapes=[pltpu.SemaphoreType.DMA],
        compiler_params=params(),
    )(stream, after)


def half_body(sibling, rows_ref, weight_ref, out_ref):
    core = place()[3]
    which = 1 - core if sibling else core
    out_ref[...] = jnp.dot(
        rows_ref[which], weight_ref[...], preferred_element_type=jnp.float32
    ).astype(jnp.bfloat16)


def half_project(sibling, rows, weight):
    return pl.pallas_call(
        functools.partial(half_body, sibling),
        out_shape=jax.ShapeDtypeStruct((rows.shape[1], weight.shape[1]), jnp.bfloat16),
        in_specs=[VMEM, VMEM],
        out_specs=VMEM,
        compiler_params=params(),
    )(rows, weight)


def relative(at):
    return [(at + 1) % SIDE, (at + 2) % SIDE, (at + 3) % SIDE, at]


def pair_body(kept_ref, came_ref, one_ref, two_ref, three_ref, own_ref):
    for at, out in zip(relative(place()[2]), (one_ref, two_ref, three_ref, own_ref)):
        out[...] = (kept_ref[at].astype(jnp.float32) + came_ref[at].astype(jnp.float32)).astype(out.dtype)


def pair(kept, came):
    part = kept.shape[0] // SIDE
    shape = (part, WIDTH)
    return pl.pallas_call(
        pair_body,
        out_shape=[jax.ShapeDtypeStruct(shape, jnp.bfloat16)] * 3
        + [jax.ShapeDtypeStruct(shape, jnp.float32)],
        in_specs=[VMEM, VMEM],
        out_specs=[VMEM] * 4,
        compiler_params=params(),
    )(kept.reshape(SIDE, part, WIDTH), came.reshape(SIDE, part, WIDTH))


def settle_body(stream_ref, own_ref, a_ref, b_ref, c_ref, out_ref):
    total = own_ref[...]
    for piece in (a_ref, b_ref, c_ref):
        total = total + piece[...].astype(jnp.float32)
    out_ref[...] = (stream_ref[...].astype(jnp.float32) + total).astype(jnp.bfloat16)


def settle(stream_rows, own, pieces):
    return pl.pallas_call(
        settle_body,
        out_shape=jax.ShapeDtypeStruct(own.shape, jnp.bfloat16),
        in_specs=[VMEM] * 5,
        out_specs=VMEM,
        compiler_params=params(),
    )(stream_rows, own, *pieces)


def lay_body(one_ref, two_ref, three_ref, own_ref, out_ref):
    for at, block in zip(relative(place()[2]), (one_ref, two_ref, three_ref, own_ref)):
        out_ref[at] = block[...]


def lay(blocks):
    return pl.pallas_call(
        lay_body,
        out_shape=jax.ShapeDtypeStruct((SIDE,) + blocks[0].shape, jnp.bfloat16),
        in_specs=[VMEM] * 4,
        out_specs=VMEM,
        compiler_params=params(),
    )(*blocks)


def scale(block, gain_ref):
    widened = block.astype(jnp.float32)
    totals = jnp.sum(widened * widened, axis=1, keepdims=True)
    scaled = (widened * gain_ref[...].astype(jnp.float32)).astype(jnp.bfloat16)
    return scaled, jnp.broadcast_to(totals, (block.shape[0], HD))


def assemble_body(this_ref, other_ref, gain_ref, residual_ref, rows_ref, squares_ref):
    core = place()[3]
    half = SIDE // 2
    for which, half_ref in ((core, this_ref), (1 - core, other_ref)):
        size = half_ref.shape[0]
        residual_ref[pl.ds(pl.multiple_of(which * size, size), size), :] = half_ref[...]
        scaled, totals = scale(half_ref[...], gain_ref)
        rows_ref[pl.ds(which * half, half)] = scaled.reshape(half, SIDE, ROWS, WIDTH)
        squares_ref[pl.ds(which * half, half)] = totals.reshape(half, SIDE, ROWS, HD)


def assemble(this_half, other_half, gain):
    return pl.pallas_call(
        assemble_body,
        out_shape=[
            jax.ShapeDtypeStruct((REQS, WIDTH), jnp.bfloat16),
            jax.ShapeDtypeStruct((SIDE, SIDE, ROWS, WIDTH), jnp.bfloat16),
            jax.ShapeDtypeStruct((SIDE, SIDE, ROWS, HD), jnp.float32),
        ],
        in_specs=[VMEM] * 3,
        out_specs=[VMEM] * 3,
        compiler_params=params(),
    )(this_half, other_half, gain)


CUTS = (0, 1664, 3328)


def part_columns(line, part):
    return CUTS[part + 1] - CUTS[part] + (HD if line and part else 0)


def project_steps(steps, parts, block_of, up_ref, gate_ref, refs):
    size = SIDE * ROWS
    refs = iter(refs)
    for line, weight_ref in ((1, gate_ref), (0, up_ref)):
        here, core = place()[line], place()[3]
        blocks = []
        for step in steps:
            there = (here + jnp.where(core == 0, SIDE - step, step)) % SIDE
            for other in range(SIDE):
                blocks.append(block_of(other, there) if line else block_of(there, other))
        lhs = jnp.concatenate([rows for rows, _ in blocks], axis=0)
        for part in parts:
            width = CUTS[part + 1] - CUTS[part]
            product = jnp.dot(
                lhs, weight_ref[:, CUTS[part] : CUTS[part + 1]], preferred_element_type=jnp.float32
            )
            for k in range(len(steps)):
                out = next(refs)
                out[:, :width] = product[size * k : size * (k + 1)].astype(out.dtype)
                if line and part:
                    totals = [t for _, t in blocks[SIDE * k : SIDE * (k + 1)]]
                    out[:, width:] = jnp.concatenate(totals, axis=0).astype(out.dtype)


def first_body(steps, parts, this_ref, other_ref, gain_ref, up_ref, gate_ref, *refs):
    core = place()[3]
    this = this_ref.reshape(SIDE // 2, SIDE, ROWS, WIDTH)
    other = other_ref.reshape(SIDE // 2, SIDE, ROWS, WIDTH)

    def block_of(i, j):
        block = jnp.where(i // 2 == core, this[i % 2, j], other[i % 2, j])
        return scale(block, gain_ref)

    project_steps(steps, parts, block_of, up_ref, gate_ref, refs)


def rest_body(steps, parts, rows_ref, squares_ref, up_ref, gate_ref, *refs):
    project_steps(steps, parts, lambda i, j: (rows_ref[i, j], squares_ref[i, j]), up_ref, gate_ref, refs)


def project(body, steps, parts, dtype, weights, *arrays):
    keys = [(line, part, step) for line in (1, 0) for part in parts for step in steps]
    results = pl.pallas_call(
        functools.partial(body, steps, parts),
        out_shape=[
            jax.ShapeDtypeStruct((SIDE * ROWS, part_columns(line, part)), dtype) for line, part, _ in keys
        ],
        in_specs=[VMEM] * (len(arrays) + 2),
        out_specs=[VMEM] * len(keys),
        compiler_params=params(24),
    )(*arrays, *weights)
    return dict(zip(keys, results))


def relay_body(own_ref, came_ref, out_ref):
    out_ref[...] = (own_ref[...] + came_ref[...].astype(jnp.float32)).astype(jnp.bfloat16)


def relay(own, came):
    return pl.pallas_call(
        relay_body,
        out_shape=jax.ShapeDtypeStruct(own.shape, jnp.bfloat16),
        in_specs=[VMEM] * 2,
        out_specs=VMEM,
        compiler_params=params(),
    )(own, came)


def merge_body(line, first_ref, second_ref, first_came, second_came, *refs):
    outs, sums_ref = refs[:4], refs[4]
    start = 0
    for own_ref, came_ref in ((first_ref, first_came), (second_ref, second_came)):
        total = own_ref[...] + came_ref[...].astype(jnp.float32)
        width = total.shape[1]
        sums_ref[:, :, start : start + width] = total.reshape(SIDE, ROWS, width)
        start += width
    for at, out in zip(relative(place()[1 - line]), outs):
        out[...] = sums_ref[at].astype(out.dtype)


def merge(line, own, came):
    columns = sum(a.shape[1] for a in own)
    return pl.pallas_call(
        functools.partial(merge_body, line),
        out_shape=[jax.ShapeDtypeStruct((ROWS, columns), jnp.bfloat16)] * 3
        + [jax.ShapeDtypeStruct((ROWS, columns), jnp.float32)],
        in_specs=[VMEM] * 4,
        out_specs=[VMEM] * 4,
        scratch_shapes=[pltpu.VMEM((SIDE, ROWS, columns), jnp.float32)],
        compiler_params=params(),
    )(*own, *came)


def along_z(x, shift):
    return lax.ppermute(
        x, "attn", [(y * SIDE + z, y * SIDE + (z + shift) % SIDE) for y in range(SIDE) for z in range(SIDE)]
    )


def along_y(x, shift):
    return lax.ppermute(
        x, "attn", [(y * SIDE + z, (y + shift) % SIDE * SIDE + z) for y in range(SIDE) for z in range(SIDE)]
    )


def along_x(x, shift):
    return lax.ppermute(
        x, "ffn", [(chip * 2 + core, (chip + shift) % SIDE * 2 + core) for chip in range(SIDE) for core in range(2)]
    )


def to_sibling(x):
    return lax.ppermute(x, "ffn", [(f, f ^ 1) for f in range(8)])


def along_ring(line, x):
    pairs = []
    for y in range(SIDE):
        for z in range(SIDE):
            for ffn in range(8):
                way = 1 - 2 * (ffn % 2)
                at = [y, z]
                at[line] = (at[line] + way) % SIDE
                pairs.append(((y * SIDE + z) * 8 + ffn, (at[0] * SIDE + at[1]) * 8 + ffn))
    return lax.ppermute(x, ("attn", "ffn"), pairs)


def scatter(halves, gain, weights):
    came = {}
    for part in range(2):
        first = project(first_body, (1,), (part,), jnp.bfloat16, weights, *halves, gain)
        for line in (1, 0):
            came[line, part] = along_ring(line, first[line, part, 1])
    residual, rows, squares = assemble(*halves, gain)
    rest = project(rest_body, (2,), (0, 1), jnp.float32, weights, rows, squares)
    rest |= project(rest_body, (3, 0), (0, 1), jnp.float32, weights, rows, squares)
    for step in (2, 3):
        for part in range(2):
            for line in (1, 0):
                came[line, part] = along_ring(line, relay(rest[line, part, step], came[line, part]))
    sums = []
    for line, cross in ((1, along_y), (0, along_z)):
        one, two, three, mine = merge(
            line, [rest[line, part, 0] for part in range(2)], [came[line, part] for part in range(2)]
        )
        sums.append((mine, cross(two, 2), cross(one, 1), cross(three, 3)))
    return residual, sums


def line_of(shift, x):
    one, three, two = shift(x, 3), shift(x, 1), shift(x, 2)
    return one, two, three, x


def on_device(
    stream,
    queries,
    k_pool,
    v_pool,
    page_table,
    lengths,
    home_device,
    w_out,
    norm_gain,
    w_gate,
    w_up,
):
    f32 = jnp.float32
    home = home_device.reshape(1, REQS)
    lengths = lengths.reshape(1, REQS)

    table = page_table.T
    outgoing, dest = dispatch(home, queries)
    listed, *here = prepare(home, lengths, table, k_pool, v_pool)
    arrived = lax.all_to_all(outgoing, "attn", split_axis=0, concat_axis=0, tiled=True)
    blended = attend(listed, arrived, *here)
    returned = lax.all_to_all(blended, "attn", split_axis=0, concat_axis=0, tiled=True)
    left, right = collect(dest, returned)
    stream_rows = own_stream(stream, left)
    left, right = gather_line(line_of(along_z, left), line_of(along_y, right))
    gathered = gather_all(line_of(along_y, left), line_of(along_z, right))
    half = REQS // 2
    gathered = gathered.reshape(2, half, HEADS * HD)

    came = to_sibling(half_project(True, gathered, w_out))
    kept = half_project(False, gathered, w_out)
    one, two, three, own = pair(kept, came)
    pieces = (along_x(two, 2), along_x(one, 1), along_x(three, 3))
    mine_rows = settle(stream_rows, own, pieces)
    first, third, second = along_x(mine_rows, 3), along_x(mine_rows, 1), along_x(mine_rows, 2)
    this_half = lay((first, second, third, mine_rows)).reshape(half, WIDTH)
    other_half = to_sibling(this_half)

    residual, sums = scatter((this_half, other_half), norm_gain.reshape(1, WIDTH), (w_up, w_gate))
    gate, up = (sum(p.astype(f32) for p in parts) for parts in sums)
    columns = w_gate.shape[1]
    scaling = lax.rsqrt(gate[:, columns : columns + 1] / D + EPS)
    gate = gate[:, :columns] * scaling
    up = up * scaling
    hidden = (jax.nn.silu(gate) * up).astype(jnp.bfloat16)
    return (residual, hidden)


def solution(mesh):
    return jax.shard_map(
        on_device,
        mesh=mesh,
        in_specs=(
            P(None, "attn"),
            P("attn", "ffn"),
            P("attn", None, "ffn"),
            P("attn", None, "ffn"),
            P(),
            P(),
            P(),
            P("ffn", "attn"),
            P("attn"),
            P("attn", "ffn"),
            P("attn", "ffn"),
        ),
        out_specs=(P(None, "attn"), P("attn", "ffn")),
        check_vma=False,
    )
```

```python
import functools
import jax
import jax.numpy as jnp
from jax import lax
from jax.experimental import pallas as pl
from jax.experimental.pallas import tpu as pltpu
from jax.sharding import PartitionSpec as P

D = 16384
HD = 128
HEADS = 16
PAGE = 16
MAXP = 32
CTX = PAGE * MAXP
REQS = 512
N_ATTN = 16
ROWS = 32
CAP = 4
SLOTS = N_ATTN * CAP
SIDE = 4
WIDTH = 1024
GROUP = 8
LISTED = 128
SHORT = MAXP // 2
EPS = 1e-05

SMEM = pl.BlockSpec(memory_space=pltpu.SMEM)
VMEM = pl.BlockSpec(memory_space=pltpu.VMEM)
HBM = pl.BlockSpec(memory_space=pltpu.HBM)


WIDE = 58


def params(mebibytes=16):
    return pltpu.CompilerParams(vmem_limit_bytes=mebibytes * 1024 * 1024)


def place():
    attn, ffn = lax.axis_index("attn"), lax.axis_index("ffn")
    return attn // SIDE, attn % SIDE, ffn // 2, ffn % 2


def stand():
    y, z, _, core = place()
    return jnp.where(core == 0, z, y), jnp.where(core == 0, y, z)


def spot(first, second):
    core = place()[3]
    return jnp.where(core == 0, second, first), jnp.where(core == 0, first, second)


def start_all(copies):
    for copy in copies:
        copy.start()
    return copies


def dispatch_body(home_hbm, queries_hbm, out_ref, dest_ref, queries_ref, tall_ref, home_ref, count_ref, sems):
    pairs = ((home_hbm, home_ref), (queries_hbm, queries_ref))
    copies = start_all([pltpu.make_async_copy(a, b, sems.at[k]) for k, (a, b) in enumerate(pairs)])
    out_ref[...] = jnp.zeros_like(out_ref)
    for target in range(N_ATTN):
        count_ref[target] = 0
    base = (lax.axis_index("attn")) * ROWS
    copies[0].wait()
    dests = []
    for row in range(ROWS):
        target = home_ref[0, base + row]
        rank = count_ref[target]
        count_ref[target] = rank + 1
        dests.append(target * CAP + rank)
        dest_ref[row] = dests[row]
    copies[1].wait()
    for head in range(HEADS):
        tall_ref[pl.ds(head, ROWS, stride=HEADS), :] = queries_ref[
            :, head * HD : (head + 1) * HD
        ].astype(jnp.float32)
    for row in range(ROWS):
        out_ref[dests[row]] = tall_ref[row * HEADS : (row + 1) * HEADS].astype(jnp.bfloat16)


def dispatch(home, queries):
    return pl.pallas_call(
        dispatch_body,
        out_shape=[
            jax.ShapeDtypeStruct((SLOTS, HEADS, HD), jnp.bfloat16),
            jax.ShapeDtypeStruct((ROWS,), jnp.int32),
        ],
        in_specs=[HBM, HBM],
        out_specs=[VMEM, SMEM],
        scratch_shapes=[
            pltpu.VMEM((ROWS, HEADS * HD), jnp.bfloat16),
            pltpu.VMEM((ROWS * HEADS, HD), jnp.float32),
            pltpu.SMEM((1, REQS), jnp.int32),
            pltpu.SMEM((N_ATTN,), jnp.int32),
            pltpu.SemaphoreType.DMA((2,)),
        ],
        compiler_params=params(WIDE),
    )(home, queries)


def prepare_body(home_hbm, lengths_hbm, list_ref, home_ref, lengths_ref, found_ref, sems):
    pairs = ((home_hbm, home_ref), (lengths_hbm, lengths_ref))
    copies = start_all([pltpu.make_async_copy(a, b, sems.at[k]) for k, (a, b) in enumerate(pairs)])
    mine = lax.axis_index("attn")
    copies[0].wait()

    def scan_source(source, found):
        for row in range(ROWS):
            request = source * ROWS + row
            found_ref[found] = request
            found = found + jnp.where(home_ref[0, request] == mine, 1, 0)
        return found

    total = lax.fori_loop(0, N_ATTN, scan_source, jnp.int32(0))
    copies[1].wait()

    def sort_entry(index, state):
        short, long, before, rank = state
        request = found_ref[index]
        source = request // ROWS
        rank = jnp.where(source == before, rank + 1, 0)
        entry = request * SLOTS + source * CAP + rank
        list_ref[0, short] = entry
        list_ref[1, long] = entry
        is_long = jnp.where(lengths_ref[0, request] > SHORT * PAGE, 1, 0)
        return short + 1 - is_long, long + is_long, source, rank

    zero = jnp.int32(0)
    counts = lax.fori_loop(0, total, sort_entry, (zero, zero, zero - 1, zero))[:2]
    for kind in range(2):
        last = list_ref[kind, jnp.maximum(counts[kind] - 1, 0)]
        for extra in range(GROUP):
            list_ref[kind, counts[kind] + extra] = last
        list_ref[kind, LISTED - 1] = counts[kind]


def prepare(home, lengths):
    return pl.pallas_call(
        prepare_body,
        out_shape=jax.ShapeDtypeStruct((2, LISTED), jnp.int32),
        in_specs=[HBM] * 2,
        out_specs=SMEM,
        scratch_shapes=[
            pltpu.SMEM(home.shape, jnp.int32),
            pltpu.SMEM(lengths.shape, jnp.int32),
            pltpu.SMEM((LISTED,), jnp.int32),
            pltpu.SemaphoreType.DMA((2,)),
        ],
        compiler_params=params(WIDE),
    )(home, lengths)


def attend_body(list_ref, queries_hbm, lengths_hbm, table_hbm, k_hbm, v_hbm, out_ref, *refs):
    queries_ref, lengths_ref, table_ref, k_ref, v_ref, sems = refs
    first, rest = pl.ds(0, SHORT), pl.ds(SHORT, MAXP - SHORT)
    pairs = (
        (lengths_hbm, lengths_ref),
        (table_hbm.at[first], table_ref.at[first]),
        (k_hbm, k_ref),
        (queries_hbm, queries_ref),
        (v_hbm, v_ref),
        (table_hbm.at[rest], table_ref.at[rest]),
    )
    copies = start_all([pltpu.make_async_copy(a, b, sems.at[k]) for k, (a, b) in enumerate(pairs)])
    out_ref[...] = jnp.zeros_like(out_ref)
    for copy in copies[:-1]:
        copy.wait()

    def step(kind, count, index, carry):
        positions = lax.broadcasted_iota(jnp.int32, (HEADS, count * PAGE), 1)
        chosen = []
        for member in range(GROUP):
            entry = list_ref[kind, index * GROUP + member]
            request, slot = entry // SLOTS, entry % SLOTS
            pages = [table_ref[page, request] for page in range(count)]
            chosen.append((request, slot, pages))
        scores = []
        for request, slot, pages in chosen:
            keys = jnp.concatenate([k_ref[page] for page in pages], axis=0)
            scores.append(
                lax.dot_general(
                    queries_ref[slot],
                    keys,
                    (((1,), (1,)), ((), ())),
                    preferred_element_type=jnp.float32,
                )
                * HD ** (-0.5)
            )
        outputs = []
        for (request, slot, pages), score in zip(chosen, scores):
            visible = positions < lengths_ref[0, request]
            maxima = jnp.max(jnp.where(visible, score, -jnp.inf), axis=1, keepdims=True)
            weights = jnp.where(visible, jnp.exp(score - maxima), 0.0)
            totals = jnp.sum(weights, axis=1, keepdims=True)
            outputs.append((weights.astype(jnp.bfloat16), totals))
        for (request, slot, pages), (weights, totals) in zip(chosen, outputs):
            values = jnp.concatenate([v_ref[page] for page in pages], axis=0)
            blended = jnp.dot(weights, values, preferred_element_type=jnp.float32)
            out_ref[slot] = (blended / totals).astype(jnp.bfloat16)
        return carry

    for kind, count in ((0, SHORT), (1, MAXP)):
        if kind:
            copies[-1].wait()
        groups = (list_ref[kind, LISTED - 1] + GROUP - 1) // GROUP
        lax.fori_loop(0, groups, functools.partial(step, kind, count), 0)


def attend(listed, queries, lengths, table, k_pool, v_pool):
    arrays = (queries, lengths, table, k_pool, v_pool)
    spaces = (pltpu.VMEM, pltpu.SMEM, pltpu.SMEM, pltpu.VMEM, pltpu.VMEM)
    return pl.pallas_call(
        attend_body,
        out_shape=jax.ShapeDtypeStruct((SLOTS, HEADS, HD), jnp.bfloat16),
        in_specs=[SMEM, pl.BlockSpec(memory_space=pl.ANY)] + [HBM] * 4,
        out_specs=VMEM,
        scratch_shapes=[space(a.shape, a.dtype) for space, a in zip(spaces, arrays)]
        + [pltpu.SemaphoreType.DMA((6,))],
        compiler_params=params(WIDE),
    )(listed, *arrays)


def collect_body(dest_hbm, slots_ref, out_ref, wide_ref, dest_ref, sem):
    pltpu.async_copy(dest_hbm, dest_ref, sem).wait()
    for row in range(ROWS):
        heads = slots_ref[dest_ref[row]].astype(jnp.float32)
        for head in range(HEADS):
            wide_ref[row : row + 1, head * HD : (head + 1) * HD] = heads[head : head + 1]
    out_ref[...] = wide_ref[...].astype(jnp.bfloat16)


def collect(dest, slots):
    return pl.pallas_call(
        collect_body,
        out_shape=jax.ShapeDtypeStruct((ROWS, HEADS * HD), jnp.bfloat16),
        in_specs=[pl.BlockSpec(memory_space=pl.ANY), VMEM],
        out_specs=VMEM,
        scratch_shapes=[
            pltpu.VMEM((ROWS, HEADS * HD), jnp.float32),
            pltpu.SMEM((ROWS,), jnp.int32),
            pltpu.SemaphoreType.DMA,
        ],
        compiler_params=params(),
    )(dest, slots)


def gather_line_body(*refs):
    for at, block in zip(relative(stand()[0]), refs[:4]):
        refs[4][at] = block[...]


def gather_line(blocks):
    return pl.pallas_call(
        gather_line_body,
        out_shape=jax.ShapeDtypeStruct((SIDE,) + blocks[0].shape, jnp.bfloat16),
        in_specs=[VMEM] * 4,
        out_specs=VMEM,
        compiler_params=params(),
    )(*blocks)


def gather_all_body(*refs):
    for at, block in zip(relative(stand()[1]), refs[:4]):
        for k in range(SIDE):
            y, z = spot(k, at)
            refs[4][y * SIDE + z] = block[k]


def gather_all(blocks):
    return pl.pallas_call(
        gather_all_body,
        out_shape=jax.ShapeDtypeStruct((N_ATTN,) + blocks[0].shape[1:], jnp.bfloat16),
        in_specs=[VMEM] * 4,
        out_specs=VMEM,
        compiler_params=params(),
    )(*blocks)


def own_stream_body(stream_hbm, after_hbm, out_ref, sem):
    part = out_ref.shape[0]
    first = pl.multiple_of(place()[3] * (SIDE * part) + place()[2] * part, part)
    pltpu.async_copy(stream_hbm.at[pl.ds(first, part)], out_ref, sem).wait()


def own_stream(stream, after):
    return pl.pallas_call(
        own_stream_body,
        out_shape=jax.ShapeDtypeStruct((REQS // 8, WIDTH), stream.dtype),
        in_specs=[HBM] * 2,
        out_specs=VMEM,
        scratch_shapes=[pltpu.SemaphoreType.DMA],
        compiler_params=params(),
    )(stream, after)


def half_body(sibling, rows_ref, weight_ref, out_ref):
    core = place()[3]
    which = 1 - core if sibling else core
    out_ref[...] = jnp.dot(
        rows_ref[which], weight_ref[...], preferred_element_type=jnp.float32
    ).astype(jnp.bfloat16)


def half_project(sibling, rows, weight):
    return pl.pallas_call(
        functools.partial(half_body, sibling),
        out_shape=jax.ShapeDtypeStruct((rows.shape[1], weight.shape[1]), jnp.bfloat16),
        in_specs=[VMEM, VMEM],
        out_specs=VMEM,
        compiler_params=params(),
    )(rows, weight)


def relative(at):
    return [(at + 1) % SIDE, (at + 2) % SIDE, (at + 3) % SIDE, at]


def pair_body(kept_ref, came_ref, one_ref, two_ref, three_ref, own_ref):
    for at, out in zip(relative(place()[2]), (one_ref, two_ref, three_ref, own_ref)):
        out[...] = (kept_ref[at].astype(jnp.float32) + came_ref[at].astype(jnp.float32)).astype(out.dtype)


def pair(kept, came):
    part = kept.shape[0] // SIDE
    shape = (part, WIDTH)
    return pl.pallas_call(
        pair_body,
        out_shape=[jax.ShapeDtypeStruct(shape, jnp.bfloat16)] * 3
        + [jax.ShapeDtypeStruct(shape, jnp.float32)],
        in_specs=[VMEM, VMEM],
        out_specs=[VMEM] * 4,
        compiler_params=params(),
    )(kept.reshape(SIDE, part, WIDTH), came.reshape(SIDE, part, WIDTH))


def settle_body(stream_ref, own_ref, a_ref, b_ref, c_ref, out_ref):
    total = own_ref[...]
    for piece in (a_ref, b_ref, c_ref):
        total = total + piece[...].astype(jnp.float32)
    out_ref[...] = (stream_ref[...].astype(jnp.float32) + total).astype(jnp.bfloat16)


def settle(stream_rows, own, pieces):
    return pl.pallas_call(
        settle_body,
        out_shape=jax.ShapeDtypeStruct(own.shape, jnp.bfloat16),
        in_specs=[VMEM] * 5,
        out_specs=VMEM,
        compiler_params=params(),
    )(stream_rows, own, *pieces)


def lay_body(one_ref, two_ref, three_ref, own_ref, out_ref):
    for at, block in zip(relative(place()[2]), (one_ref, two_ref, three_ref, own_ref)):
        out_ref[at] = block[...]


def lay(blocks):
    return pl.pallas_call(
        lay_body,
        out_shape=jax.ShapeDtypeStruct((SIDE,) + blocks[0].shape, jnp.bfloat16),
        in_specs=[VMEM] * 4,
        out_specs=VMEM,
        compiler_params=params(),
    )(*blocks)


def scale(block, gain_ref):
    widened = block.astype(jnp.float32)
    totals = jnp.sum(widened * widened, axis=1, keepdims=True)
    scaled = (widened * gain_ref[...].astype(jnp.float32)).astype(jnp.bfloat16)
    return scaled, jnp.broadcast_to(totals, (block.shape[0], HD))


def assemble_body(this_ref, other_ref, gain_ref, residual_ref, rows_ref, squares_ref):
    core = place()[3]
    half = SIDE // 2
    for which, half_ref in ((core, this_ref), (1 - core, other_ref)):
        size = half_ref.shape[0]
        residual_ref[pl.ds(pl.multiple_of(which * size, size), size), :] = half_ref[...]
        scaled, totals = scale(half_ref[...], gain_ref)
        rows_ref[pl.ds(which * half, half)] = scaled.reshape(half, SIDE, ROWS, WIDTH)
        squares_ref[pl.ds(which * half, half)] = totals.reshape(half, SIDE, ROWS, HD)


def assemble(this_half, other_half, gain):
    return pl.pallas_call(
        assemble_body,
        out_shape=[
            jax.ShapeDtypeStruct((REQS, WIDTH), jnp.bfloat16),
            jax.ShapeDtypeStruct((SIDE, SIDE, ROWS, WIDTH), jnp.bfloat16),
            jax.ShapeDtypeStruct((SIDE, SIDE, ROWS, HD), jnp.float32),
        ],
        in_specs=[VMEM] * 3,
        out_specs=[VMEM] * 3,
        compiler_params=params(),
    )(this_half, other_half, gain)


CUTS = (0, 1664, 3328)


def part_columns(kind, part):
    return CUTS[part + 1] - CUTS[part] + (HD if kind and part else 0)


def project_steps(steps, parts, block_of, up_ref, gate_ref, refs):
    size = SIDE * ROWS
    refs = iter(refs)
    here = stand()[0]
    for kind, weight_ref in ((1, gate_ref), (0, up_ref)):
        blocks = []
        for step in steps:
            there = (here + (SIDE - step if kind else step)) % SIDE
            for other in range(SIDE):
                blocks.append(block_of(*spot(there, other)))
        lhs = jnp.concatenate([rows for rows, _ in blocks], axis=0)
        for part in parts:
            width = CUTS[part + 1] - CUTS[part]
            product = jnp.dot(
                lhs, weight_ref[:, CUTS[part] : CUTS[part + 1]], preferred_element_type=jnp.float32
            )
            for k in range(len(steps)):
                out = next(refs)
                out[:, :width] = product[size * k : size * (k + 1)].astype(out.dtype)
                if kind and part:
                    totals = [t for _, t in blocks[SIDE * k : SIDE * (k + 1)]]
                    out[:, width:] = jnp.concatenate(totals, axis=0).astype(out.dtype)


def first_body(steps, parts, this_ref, other_ref, gain_ref, up_ref, gate_ref, *refs):
    core = place()[3]
    this = this_ref.reshape(SIDE // 2, SIDE, ROWS, WIDTH)
    other = other_ref.reshape(SIDE // 2, SIDE, ROWS, WIDTH)

    def block_of(i, j):
        block = jnp.where(i // 2 == core, this[i % 2, j], other[i % 2, j])
        return scale(block, gain_ref)

    project_steps(steps, parts, block_of, up_ref, gate_ref, refs)


def rest_body(steps, parts, rows_ref, squares_ref, up_ref, gate_ref, *refs):
    project_steps(steps, parts, lambda i, j: (rows_ref[i, j], squares_ref[i, j]), up_ref, gate_ref, refs)


def project(body, steps, parts, dtype, weights, *arrays):
    keys = [(kind, part, step) for kind in (1, 0) for part in parts for step in steps]
    results = pl.pallas_call(
        functools.partial(body, steps, parts),
        out_shape=[
            jax.ShapeDtypeStruct((SIDE * ROWS, part_columns(kind, part)), dtype) for kind, part, _ in keys
        ],
        in_specs=[VMEM] * (len(arrays) + 2),
        out_specs=[VMEM] * len(keys),
        compiler_params=params(24),
    )(*arrays, *weights)
    return dict(zip(keys, results))


def relay_body(own_ref, came_ref, out_ref):
    out_ref[...] = (own_ref[...] + came_ref[...].astype(jnp.float32)).astype(jnp.bfloat16)


def relay(own, came):
    return pl.pallas_call(
        relay_body,
        out_shape=jax.ShapeDtypeStruct(own.shape, jnp.bfloat16),
        in_specs=[VMEM] * 2,
        out_specs=VMEM,
        compiler_params=params(),
    )(own, came)


def merge_body(*refs):
    outs, sums_ref = refs[8:12], refs[12]
    start = 0
    for own_ref, came_ref in zip(refs[:4], refs[4:8]):
        total = own_ref[...] + came_ref[...].astype(jnp.float32)
        width = total.shape[1]
        sums_ref[:, :, start : start + width] = total.reshape(SIDE, ROWS, width)
        start += width
    for at, out in zip(relative(stand()[1]), outs):
        out[...] = sums_ref[at].astype(out.dtype)


def merge(own, came):
    columns = sum(a.shape[1] for a in own)
    return pl.pallas_call(
        merge_body,
        out_shape=[jax.ShapeDtypeStruct((ROWS, columns), jnp.bfloat16)] * 3
        + [jax.ShapeDtypeStruct((ROWS, columns), jnp.float32)],
        in_specs=[VMEM] * 8,
        out_specs=[VMEM] * 4,
        scratch_shapes=[pltpu.VMEM((SIDE, ROWS, columns), jnp.float32)],
        compiler_params=params(24),
    )(*own, *came)


def along(second, x, shift):
    pairs = []
    for y in range(SIDE):
        for z in range(SIDE):
            for ffn in range(8):
                at = [y, z]
                line = (1 - ffn % 2) ^ second
                at[line] = (at[line] + shift) % SIDE
                pairs.append(((y * SIDE + z) * 8 + ffn, (at[0] * SIDE + at[1]) * 8 + ffn))
    return lax.ppermute(x, ("attn", "ffn"), pairs)


def along_x(x, shift):
    return lax.ppermute(
        x, "ffn", [(chip * 2 + core, (chip + shift) % SIDE * 2 + core) for chip in range(SIDE) for core in range(2)]
    )


def to_sibling(x):
    return lax.ppermute(x, "ffn", [(f, f ^ 1) for f in range(8)])


def scatter(halves, gain, weights):
    came = {}
    keys = [(kind, part) for part in range(2) for kind in (1, 0)]

    def send(kind, x):
        return along(0, x, 1 if kind else 3)

    for part in range(2):
        first = project(first_body, (1,), (part,), jnp.bfloat16, weights, *halves, gain)
        for kind in (1, 0):
            came[kind, part] = send(kind, first[kind, part, 1])
    residual, rows, squares = assemble(*halves, gain)
    rest = project(rest_body, (2,), (0, 1), jnp.float32, weights, rows, squares)
    rest |= project(rest_body, (3, 0), (0, 1), jnp.float32, weights, rows, squares)
    for step in (2, 3):
        for kind, part in keys:
            came[kind, part] = send(kind, relay(rest[kind, part, step], came[kind, part]))
    order = ((1, 0), (1, 1), (0, 0), (0, 1))
    one, two, three, mine = merge([rest[key + (0,)] for key in order], [came[key] for key in order])
    return residual, (mine, along(1, two, 2), along(1, one, 1), along(1, three, 3))


def line_of(second, x):
    one, three, two = along(second, x, 3), along(second, x, 1), along(second, x, 2)
    return one, two, three, x


def on_device(
    stream,
    queries,
    k_pool,
    v_pool,
    page_table,
    lengths,
    home_device,
    w_out,
    norm_gain,
    w_gate,
    w_up,
):
    f32 = jnp.float32
    home = home_device.reshape(1, REQS)
    lengths = lengths.reshape(1, REQS)

    table = page_table.T
    outgoing, dest = dispatch(home, queries)
    listed = prepare(home, lengths)
    arrived = lax.all_to_all(outgoing, "attn", split_axis=0, concat_axis=0, tiled=True)
    blended = attend(listed, arrived, lengths, table, k_pool, v_pool)
    returned = lax.all_to_all(blended, "attn", split_axis=0, concat_axis=0, tiled=True)
    attention = collect(dest, returned)
    stream_rows = own_stream(stream, attention)
    gathered = gather_all(line_of(1, gather_line(line_of(0, attention))))
    half = REQS // 2
    gathered = gathered.reshape(2, half, HEADS * HD)

    came = to_sibling(half_project(True, gathered, w_out))
    kept = half_project(False, gathered, w_out)
    one, two, three, own = pair(kept, came)
    pieces = (along_x(two, 2), along_x(one, 1), along_x(three, 3))
    mine_rows = settle(stream_rows, own, pieces)
    first, third, second = along_x(mine_rows, 3), along_x(mine_rows, 1), along_x(mine_rows, 2)
    this_half = lay((first, second, third, mine_rows)).reshape(half, WIDTH)
    other_half = to_sibling(this_half)

    residual, sums = scatter((this_half, other_half), norm_gain.reshape(1, WIDTH), (w_up, w_gate))
    total = sum(part.astype(f32) for part in sums)
    columns = w_gate.shape[1]
    scaling = lax.rsqrt(total[:, columns : columns + 1] / D + EPS)
    gate = total[:, :columns] * scaling
    up = total[:, columns + HD :] * scaling
    hidden = (jax.nn.silu(gate) * up).astype(jnp.bfloat16)
    return (residual, hidden)


def solution(mesh):
    return jax.shard_map(
        on_device,
        mesh=mesh,
        in_specs=(
            P(None, "attn"),
            P("attn", "ffn"),
            P("attn", None, "ffn"),
            P("attn", None, "ffn"),
            P(),
            P(),
            P(),
            P("ffn", "attn"),
            P("attn"),
            P("attn", "ffn"),
            P("attn", "ffn"),
        ),
        out_specs=(P(None, "attn"), P("attn", "ffn")),
        check_vma=False,
    )
```

```python
import functools
import jax
import jax.numpy as jnp
from jax import lax
from jax.experimental import pallas as pl
from jax.experimental.pallas import tpu as pltpu
from jax.sharding import PartitionSpec as P

D = 16384
HD = 128
HEADS = 16
PAGE = 16
MAXP = 32
CTX = PAGE * MAXP
REQS = 512
N_ATTN = 16
ROWS = 32
CAP = 4
SLOTS = N_ATTN * CAP
SIDE = 4
WIDTH = 1024
GROUP = 8
LISTED = 128
SHORT = MAXP // 2
EPS = 1e-05

SMEM = pl.BlockSpec(memory_space=pltpu.SMEM)
VMEM = pl.BlockSpec(memory_space=pltpu.VMEM)
HBM = pl.BlockSpec(memory_space=pltpu.HBM)


WIDE = 58


def params(mebibytes=16):
    return pltpu.CompilerParams(vmem_limit_bytes=mebibytes * 1024 * 1024)


def place():
    attn, ffn = lax.axis_index("attn"), lax.axis_index("ffn")
    return attn // SIDE, attn % SIDE, ffn // 2, ffn % 2


def stand():
    y, z, _, core = place()
    return jnp.where(core == 0, z, y), jnp.where(core == 0, y, z)


def spot(first, second):
    core = place()[3]
    return jnp.where(core == 0, second, first), jnp.where(core == 0, first, second)


def start_all(copies):
    for copy in copies:
        copy.start()
    return copies


def dispatch_body(home_hbm, queries_hbm, out_ref, dest_ref, queries_ref, tall_ref, home_ref, count_ref, sems):
    pairs = ((home_hbm, home_ref), (queries_hbm, queries_ref))
    copies = start_all([pltpu.make_async_copy(a, b, sems.at[k]) for k, (a, b) in enumerate(pairs)])
    out_ref[...] = jnp.zeros_like(out_ref)
    for target in range(N_ATTN):
        count_ref[target] = 0
    base = (lax.axis_index("attn")) * ROWS
    copies[0].wait()
    dests = []
    for row in range(ROWS):
        target = home_ref[0, base + row]
        rank = count_ref[target]
        count_ref[target] = rank + 1
        dests.append(target * CAP + rank)
        dest_ref[row] = dests[row]
    copies[1].wait()
    for head in range(HEADS):
        tall_ref[pl.ds(head, ROWS, stride=HEADS), :] = queries_ref[
            :, head * HD : (head + 1) * HD
        ].astype(jnp.float32)
    for row in range(ROWS):
        out_ref[dests[row]] = tall_ref[row * HEADS : (row + 1) * HEADS].astype(jnp.bfloat16)


def dispatch(home, queries):
    return pl.pallas_call(
        dispatch_body,
        out_shape=[
            jax.ShapeDtypeStruct((SLOTS, HEADS, HD), jnp.bfloat16),
            jax.ShapeDtypeStruct((ROWS,), jnp.int32),
        ],
        in_specs=[HBM, HBM],
        out_specs=[VMEM, SMEM],
        scratch_shapes=[
            pltpu.VMEM((ROWS, HEADS * HD), jnp.bfloat16),
            pltpu.VMEM((ROWS * HEADS, HD), jnp.float32),
            pltpu.SMEM((1, REQS), jnp.int32),
            pltpu.SMEM((N_ATTN,), jnp.int32),
            pltpu.SemaphoreType.DMA((2,)),
        ],
        compiler_params=params(WIDE),
    )(home, queries)


def prepare_body(home_hbm, lengths_hbm, list_ref, home_ref, lengths_ref, found_ref, sems):
    pairs = ((home_hbm, home_ref), (lengths_hbm, lengths_ref))
    copies = start_all([pltpu.make_async_copy(a, b, sems.at[k]) for k, (a, b) in enumerate(pairs)])
    mine = lax.axis_index("attn")
    copies[0].wait()

    def scan_source(source, found):
        for row in range(ROWS):
            request = source * ROWS + row
            found_ref[found] = request
            found = found + jnp.where(home_ref[0, request] == mine, 1, 0)
        return found

    total = lax.fori_loop(0, N_ATTN, scan_source, jnp.int32(0))
    copies[1].wait()

    def sort_entry(index, state):
        short, long, before, rank = state
        request = found_ref[index]
        source = request // ROWS
        rank = jnp.where(source == before, rank + 1, 0)
        entry = request * SLOTS + source * CAP + rank
        list_ref[0, short] = entry
        list_ref[1, long] = entry
        is_long = jnp.where(lengths_ref[0, request] > SHORT * PAGE, 1, 0)
        return short + 1 - is_long, long + is_long, source, rank

    zero = jnp.int32(0)
    counts = lax.fori_loop(0, total, sort_entry, (zero, zero, zero - 1, zero))[:2]
    for kind in range(2):
        last = list_ref[kind, jnp.maximum(counts[kind] - 1, 0)]
        for extra in range(GROUP):
            list_ref[kind, counts[kind] + extra] = last
        list_ref[kind, LISTED - 1] = counts[kind]


def prepare(home, lengths):
    return pl.pallas_call(
        prepare_body,
        out_shape=jax.ShapeDtypeStruct((2, LISTED), jnp.int32),
        in_specs=[HBM] * 2,
        out_specs=SMEM,
        scratch_shapes=[
            pltpu.SMEM(home.shape, jnp.int32),
            pltpu.SMEM(lengths.shape, jnp.int32),
            pltpu.SMEM((LISTED,), jnp.int32),
            pltpu.SemaphoreType.DMA((2,)),
        ],
        compiler_params=params(WIDE),
    )(home, lengths)


def attend_body(list_ref, queries_hbm, lengths_hbm, table_hbm, k_hbm, v_hbm, out_ref, *refs):
    queries_ref, lengths_ref, table_ref, k_ref, v_ref, sems = refs
    first, rest = pl.ds(0, SHORT), pl.ds(SHORT, MAXP - SHORT)
    pairs = (
        (lengths_hbm, lengths_ref),
        (table_hbm.at[first], table_ref.at[first]),
        (k_hbm, k_ref),
        (queries_hbm, queries_ref),
        (v_hbm, v_ref),
        (table_hbm.at[rest], table_ref.at[rest]),
    )
    copies = start_all([pltpu.make_async_copy(a, b, sems.at[k]) for k, (a, b) in enumerate(pairs)])
    out_ref[...] = jnp.zeros_like(out_ref)
    for copy in copies[:-1]:
        copy.wait()

    def step(kind, count, index, carry):
        positions = lax.broadcasted_iota(jnp.int32, (HEADS, count * PAGE), 1)
        chosen = []
        for member in range(GROUP):
            entry = list_ref[kind, index * GROUP + member]
            request, slot = entry // SLOTS, entry % SLOTS
            pages = [table_ref[page, request] for page in range(count)]
            chosen.append((request, slot, pages))
        scores = []
        for request, slot, pages in chosen:
            keys = jnp.concatenate([k_ref[page] for page in pages], axis=0)
            scores.append(
                lax.dot_general(
                    queries_ref[slot],
                    keys,
                    (((1,), (1,)), ((), ())),
                    preferred_element_type=jnp.float32,
                )
                * HD ** (-0.5)
            )
        outputs = []
        for (request, slot, pages), score in zip(chosen, scores):
            visible = positions < lengths_ref[0, request]
            maxima = jnp.max(jnp.where(visible, score, -jnp.inf), axis=1, keepdims=True)
            weights = jnp.where(visible, jnp.exp(score - maxima), 0.0)
            totals = jnp.sum(weights, axis=1, keepdims=True)
            outputs.append((weights.astype(jnp.bfloat16), totals))
        for (request, slot, pages), (weights, totals) in zip(chosen, outputs):
            values = jnp.concatenate([v_ref[page] for page in pages], axis=0)
            blended = jnp.dot(weights, values, preferred_element_type=jnp.float32)
            out_ref[slot] = (blended / totals).astype(jnp.bfloat16)
        return carry

    for kind, count in ((0, SHORT), (1, MAXP)):
        if kind:
            copies[-1].wait()
        groups = (list_ref[kind, LISTED - 1] + GROUP - 1) // GROUP
        lax.fori_loop(0, groups, functools.partial(step, kind, count), 0)


def attend(listed, queries, lengths, table, k_pool, v_pool):
    arrays = (queries, lengths, table, k_pool, v_pool)
    spaces = (pltpu.VMEM, pltpu.SMEM, pltpu.SMEM, pltpu.VMEM, pltpu.VMEM)
    return pl.pallas_call(
        attend_body,
        out_shape=jax.ShapeDtypeStruct((SLOTS, HEADS, HD), jnp.bfloat16),
        in_specs=[SMEM, pl.BlockSpec(memory_space=pl.ANY)] + [HBM] * 4,
        out_specs=VMEM,
        scratch_shapes=[space(a.shape, a.dtype) for space, a in zip(spaces, arrays)]
        + [pltpu.SemaphoreType.DMA((6,))],
        compiler_params=params(WIDE),
    )(listed, *arrays)


def collect_body(dest_hbm, slots_ref, out_ref, wide_ref, dest_ref, sem):
    pltpu.async_copy(dest_hbm, dest_ref, sem).wait()
    for row in range(ROWS):
        heads = slots_ref[dest_ref[row]].astype(jnp.float32)
        for head in range(HEADS):
            wide_ref[row : row + 1, head * HD : (head + 1) * HD] = heads[head : head + 1]
    out_ref[...] = wide_ref[...].astype(jnp.bfloat16)


def collect(dest, slots):
    return pl.pallas_call(
        collect_body,
        out_shape=jax.ShapeDtypeStruct((ROWS, HEADS * HD), jnp.bfloat16),
        in_specs=[pl.BlockSpec(memory_space=pl.ANY), VMEM],
        out_specs=VMEM,
        scratch_shapes=[
            pltpu.VMEM((ROWS, HEADS * HD), jnp.float32),
            pltpu.SMEM((ROWS,), jnp.int32),
            pltpu.SemaphoreType.DMA,
        ],
        compiler_params=params(),
    )(dest, slots)


def gather_line_body(*refs):
    for at, block in zip(relative(stand()[0]), refs[:4]):
        refs[4][at] = block[...]


def gather_line(blocks):
    return pl.pallas_call(
        gather_line_body,
        out_shape=jax.ShapeDtypeStruct((SIDE,) + blocks[0].shape, jnp.bfloat16),
        in_specs=[VMEM] * 4,
        out_specs=VMEM,
        compiler_params=params(),
    )(*blocks)


def gather_all_body(*refs):
    for at, block in zip(relative(stand()[1]), refs[:4]):
        for k in range(SIDE):
            y, z = spot(k, at)
            refs[4][y * SIDE + z] = block[k]


def gather_all(blocks):
    return pl.pallas_call(
        gather_all_body,
        out_shape=jax.ShapeDtypeStruct((N_ATTN,) + blocks[0].shape[1:], jnp.bfloat16),
        in_specs=[VMEM] * 4,
        out_specs=VMEM,
        compiler_params=params(),
    )(*blocks)


def own_stream_body(stream_hbm, after_hbm, out_ref, sem):
    part = out_ref.shape[0]
    first = pl.multiple_of(place()[3] * (SIDE * part) + place()[2] * part, part)
    pltpu.async_copy(stream_hbm.at[pl.ds(first, part)], out_ref, sem).wait()


def own_stream(stream, after):
    return pl.pallas_call(
        own_stream_body,
        out_shape=jax.ShapeDtypeStruct((REQS // 8, WIDTH), stream.dtype),
        in_specs=[HBM] * 2,
        out_specs=VMEM,
        scratch_shapes=[pltpu.SemaphoreType.DMA],
        compiler_params=params(),
    )(stream, after)


def half_body(sibling, rows_ref, weight_ref, out_ref):
    core = place()[3]
    which = 1 - core if sibling else core
    out_ref[...] = jnp.dot(
        rows_ref[which], weight_ref[...], preferred_element_type=jnp.float32
    ).astype(jnp.bfloat16)


def half_project(sibling, rows, weight):
    return pl.pallas_call(
        functools.partial(half_body, sibling),
        out_shape=jax.ShapeDtypeStruct((rows.shape[1], weight.shape[1]), jnp.bfloat16),
        in_specs=[VMEM, VMEM],
        out_specs=VMEM,
        compiler_params=params(),
    )(rows, weight)


def relative(at):
    return [(at + 1) % SIDE, (at + 2) % SIDE, (at + 3) % SIDE, at]


def pair_body(kept_ref, came_ref, one_ref, two_ref, three_ref, own_ref):
    for at, out in zip(relative(place()[2]), (one_ref, two_ref, three_ref, own_ref)):
        out[...] = (kept_ref[at].astype(jnp.float32) + came_ref[at].astype(jnp.float32)).astype(out.dtype)


def pair(kept, came):
    part = kept.shape[0] // SIDE
    shape = (part, WIDTH)
    return pl.pallas_call(
        pair_body,
        out_shape=[jax.ShapeDtypeStruct(shape, jnp.bfloat16)] * 3
        + [jax.ShapeDtypeStruct(shape, jnp.float32)],
        in_specs=[VMEM, VMEM],
        out_specs=[VMEM] * 4,
        compiler_params=params(),
    )(kept.reshape(SIDE, part, WIDTH), came.reshape(SIDE, part, WIDTH))


def settle_body(stream_ref, own_ref, a_ref, b_ref, c_ref, out_ref):
    total = own_ref[...]
    for piece in (a_ref, b_ref, c_ref):
        total = total + piece[...].astype(jnp.float32)
    out_ref[...] = (stream_ref[...].astype(jnp.float32) + total).astype(jnp.bfloat16)


def settle(stream_rows, own, pieces):
    return pl.pallas_call(
        settle_body,
        out_shape=jax.ShapeDtypeStruct(own.shape, jnp.bfloat16),
        in_specs=[VMEM] * 5,
        out_specs=VMEM,
        compiler_params=params(),
    )(stream_rows, own, *pieces)


def lay_body(one_ref, two_ref, three_ref, own_ref, out_ref):
    for at, block in zip(relative(place()[2]), (one_ref, two_ref, three_ref, own_ref)):
        out_ref[at] = block[...]


def lay(blocks):
    return pl.pallas_call(
        lay_body,
        out_shape=jax.ShapeDtypeStruct((SIDE,) + blocks[0].shape, jnp.bfloat16),
        in_specs=[VMEM] * 4,
        out_specs=VMEM,
        compiler_params=params(),
    )(*blocks)


def scale(block, gain_ref):
    widened = block.astype(jnp.float32)
    totals = jnp.sum(widened * widened, axis=1, keepdims=True)
    scaled = (widened * gain_ref[...].astype(jnp.float32)).astype(jnp.bfloat16)
    return scaled, jnp.broadcast_to(totals, (block.shape[0], HD))


def assemble_body(this_ref, other_ref, gain_ref, residual_ref, rows_ref, squares_ref):
    core = place()[3]
    half = SIDE // 2
    for which, half_ref in ((core, this_ref), (1 - core, other_ref)):
        size = half_ref.shape[0]
        residual_ref[pl.ds(pl.multiple_of(which * size, size), size), :] = half_ref[...]
        scaled, totals = scale(half_ref[...], gain_ref)
        rows_ref[pl.ds(which * half, half)] = scaled.reshape(half, SIDE, ROWS, WIDTH)
        squares_ref[pl.ds(which * half, half)] = totals.reshape(half, SIDE, ROWS, HD)


def assemble(this_half, other_half, gain):
    return pl.pallas_call(
        assemble_body,
        out_shape=[
            jax.ShapeDtypeStruct((REQS, WIDTH), jnp.bfloat16),
            jax.ShapeDtypeStruct((SIDE, SIDE, ROWS, WIDTH), jnp.bfloat16),
            jax.ShapeDtypeStruct((SIDE, SIDE, ROWS, HD), jnp.float32),
        ],
        in_specs=[VMEM] * 3,
        out_specs=[VMEM] * 3,
        compiler_params=params(),
    )(this_half, other_half, gain)


CUTS = (0, 1664, 3328)


def part_columns(kind, part):
    return CUTS[part + 1] - CUTS[part] + (HD if kind and part else 0)


def project_steps(kinds, steps, parts, block_of, weights, refs):
    size = SIDE * ROWS
    refs = iter(refs)
    here = stand()[0]
    for kind, weight_ref in zip(kinds, weights):
        blocks = []
        for step in steps:
            there = (here + (SIDE - step if kind else step)) % SIDE
            for other in range(SIDE):
                blocks.append(block_of(*spot(there, other)))
        lhs = jnp.concatenate([rows for rows, _ in blocks], axis=0)
        for part in parts:
            width = CUTS[part + 1] - CUTS[part]
            product = jnp.dot(
                lhs, weight_ref[:, CUTS[part] : CUTS[part + 1]], preferred_element_type=jnp.float32
            )
            for k in range(len(steps)):
                out = next(refs)
                out[:, :width] = product[size * k : size * (k + 1)].astype(out.dtype)
                if kind and part:
                    totals = [t for _, t in blocks[SIDE * k : SIDE * (k + 1)]]
                    out[:, width:] = jnp.concatenate(totals, axis=0).astype(out.dtype)


def first_body(kinds, steps, parts, this_ref, other_ref, gain_ref, *refs):
    core = place()[3]
    this = this_ref.reshape(SIDE // 2, SIDE, ROWS, WIDTH)
    other = other_ref.reshape(SIDE // 2, SIDE, ROWS, WIDTH)

    def block_of(i, j):
        block = jnp.where(i // 2 == core, this[i % 2, j], other[i % 2, j])
        return scale(block, gain_ref)

    project_steps(kinds, steps, parts, block_of, refs[: len(kinds)], refs[len(kinds) :])


def rest_body(kinds, steps, parts, rows_ref, squares_ref, *refs):
    project_steps(
        kinds,
        steps,
        parts,
        lambda i, j: (rows_ref[i, j], squares_ref[i, j]),
        refs[: len(kinds)],
        refs[len(kinds) :],
    )


def project(body, kinds, steps, parts, dtype, weights, *arrays):
    weights = [weights[kind] for kind in kinds]
    keys = [(kind, part, step) for kind in kinds for part in parts for step in steps]
    results = pl.pallas_call(
        functools.partial(body, kinds, steps, parts),
        out_shape=[
            jax.ShapeDtypeStruct((SIDE * ROWS, part_columns(kind, part)), dtype) for kind, part, _ in keys
        ],
        in_specs=[VMEM] * (len(arrays) + len(kinds)),
        out_specs=[VMEM] * len(keys),
        compiler_params=params(24),
    )(*arrays, *weights)
    return dict(zip(keys, results))


def relay_body(own_ref, came_ref, out_ref):
    out_ref[...] = (own_ref[...] + came_ref[...].astype(jnp.float32)).astype(jnp.bfloat16)


def relay(own, came):
    return pl.pallas_call(
        relay_body,
        out_shape=jax.ShapeDtypeStruct(own.shape, jnp.bfloat16),
        in_specs=[VMEM] * 2,
        out_specs=VMEM,
        compiler_params=params(),
    )(own, came)


def merge_body(*refs):
    outs, sums_ref = refs[8:12], refs[12]
    start = 0
    for own_ref, came_ref in zip(refs[:4], refs[4:8]):
        total = own_ref[...] + came_ref[...].astype(jnp.float32)
        width = total.shape[1]
        sums_ref[:, :, start : start + width] = total.reshape(SIDE, ROWS, width)
        start += width
    for at, out in zip(relative(stand()[1]), outs):
        out[...] = sums_ref[at].astype(out.dtype)


def merge(own, came):
    columns = sum(a.shape[1] for a in own)
    return pl.pallas_call(
        merge_body,
        out_shape=[jax.ShapeDtypeStruct((ROWS, columns), jnp.bfloat16)] * 3
        + [jax.ShapeDtypeStruct((ROWS, columns), jnp.float32)],
        in_specs=[VMEM] * 8,
        out_specs=[VMEM] * 4,
        scratch_shapes=[pltpu.VMEM((SIDE, ROWS, columns), jnp.float32)],
        compiler_params=params(24),
    )(*own, *came)


def along(second, x, shift):
    pairs = []
    for y in range(SIDE):
        for z in range(SIDE):
            for ffn in range(8):
                at = [y, z]
                line = (1 - ffn % 2) ^ second
                at[line] = (at[line] + shift) % SIDE
                pairs.append(((y * SIDE + z) * 8 + ffn, (at[0] * SIDE + at[1]) * 8 + ffn))
    return lax.ppermute(x, ("attn", "ffn"), pairs)


def along_x(x, shift):
    return lax.ppermute(
        x, "ffn", [(chip * 2 + core, (chip + shift) % SIDE * 2 + core) for chip in range(SIDE) for core in range(2)]
    )


def to_sibling(x):
    return lax.ppermute(x, "ffn", [(f, f ^ 1) for f in range(8)])


def scatter(halves, gain, weights):
    came = {}
    keys = [(kind, part) for part in range(2) for kind in (1, 0)]

    def send(kind, x):
        return along(0, x, 1 if kind else 3)

    for kind in (1, 0):
        first = project(first_body, (kind,), (1,), (0, 1), jnp.bfloat16, weights, *halves, gain)
        for part in range(2):
            came[kind, part] = send(kind, first[kind, part, 1])
    residual, rows, squares = assemble(*halves, gain)
    rest = project(rest_body, (1, 0), (2,), (0, 1), jnp.float32, weights, rows, squares)
    rest |= project(rest_body, (1, 0), (3, 0), (0, 1), jnp.float32, weights, rows, squares)
    for step in (2, 3):
        for kind, part in keys:
            came[kind, part] = send(kind, relay(rest[kind, part, step], came[kind, part]))
    order = ((1, 0), (1, 1), (0, 0), (0, 1))
    one, two, three, mine = merge([rest[key + (0,)] for key in order], [came[key] for key in order])
    return residual, (mine, along(1, two, 2), along(1, one, 1), along(1, three, 3))


def line_of(second, x):
    one, three, two = along(second, x, 3), along(second, x, 1), along(second, x, 2)
    return one, two, three, x


def on_device(
    stream,
    queries,
    k_pool,
    v_pool,
    page_table,
    lengths,
    home_device,
    w_out,
    norm_gain,
    w_gate,
    w_up,
):
    f32 = jnp.float32
    home = home_device.reshape(1, REQS)
    lengths = lengths.reshape(1, REQS)

    table = page_table.T
    outgoing, dest = dispatch(home, queries)
    listed = prepare(home, lengths)
    arrived = lax.all_to_all(outgoing, "attn", split_axis=0, concat_axis=0, tiled=True)
    blended = attend(listed, arrived, lengths, table, k_pool, v_pool)
    returned = lax.all_to_all(blended, "attn", split_axis=0, concat_axis=0, tiled=True)
    attention = collect(dest, returned)
    stream_rows = own_stream(stream, attention)
    gathered = gather_all(line_of(1, gather_line(line_of(0, attention))))
    half = REQS // 2
    gathered = gathered.reshape(2, half, HEADS * HD)

    came = to_sibling(half_project(True, gathered, w_out))
    kept = half_project(False, gathered, w_out)
    one, two, three, own = pair(kept, came)
    pieces = (along_x(two, 2), along_x(one, 1), along_x(three, 3))
    mine_rows = settle(stream_rows, own, pieces)
    first, third, second = along_x(mine_rows, 3), along_x(mine_rows, 1), along_x(mine_rows, 2)
    this_half = lay((first, second, third, mine_rows)).reshape(half, WIDTH)
    other_half = to_sibling(this_half)

    residual, sums = scatter((this_half, other_half), norm_gain.reshape(1, WIDTH), (w_up, w_gate))
    total = sum(part.astype(f32) for part in sums)
    columns = w_gate.shape[1]
    scaling = lax.rsqrt(total[:, columns : columns + 1] / D + EPS)
    gate = total[:, :columns] * scaling
    up = total[:, columns + HD :] * scaling
    hidden = (jax.nn.silu(gate) * up).astype(jnp.bfloat16)
    return (residual, hidden)


def solution(mesh):
    return jax.shard_map(
        on_device,
        mesh=mesh,
        in_specs=(
            P(None, "attn"),
            P("attn", "ffn"),
            P("attn", None, "ffn"),
            P("attn", None, "ffn"),
            P(),
            P(),
            P(),
            P("ffn", "attn"),
            P("attn"),
            P("attn", "ffn"),
            P("attn", "ffn"),
        ),
        out_specs=(P(None, "attn"), P("attn", "ffn")),
        check_vma=False,
    )
```
